32 devices in a mesh: rows: 8 (over z, x), segment: 2 (over y), chan: 2 (over core).
Axes of the slice: x: 2, y: 2, z: 4, core: 2. Of those that a mesh axis runs over, the one named last changes fastest.
Arguments:
- features: bfloat16 [4, 8, 384, 128], P(None, 'rows', 'chan'), may hold values from -6 to 6
- caches: bfloat16 [2, 2, 2, 8, 384, 128], P('segment', None, None, 'rows', 'chan'), may hold values from -4 to 4
- conv_weights: bfloat16 [2, 2, 384, 3, 3, 3, 384], P('segment', None, 'chan'), may hold values from -0.0625 to 0.0625
- conv_bias: float32 [2, 2, 384], P('segment'), may hold values from -3 to 3
- norm_gain: float32 [2, 2, 384], P('segment'), may hold values from 0.25 to 1.75
Outputs:
- section_outputs: bfloat16 [2, 4, 8, 384, 128], P('segment', None, 'rows', 'chan')
- next_caches: bfloat16 [2, 2, 2, 8, 384, 128], P('segment', None, None, 'rows', 'chan')
The draws below stay inside these ranges and needn't reach their ends.
All inputs are finite; a program needn't handle non-finite values.
Results may differ from the reference program's by a relative error of at most 0.0057.
Values may be sent and summed in bfloat16 or wider, within the bound.
No kernel may reach another device: no remote copies, remote signals or barrier semaphores. Data moves between devices by JAX's collectives and lax.ppermute only.
A program may use at most 64 MiB of HBM per device.

```python
import jax
import jax.numpy as jnp
from jax import lax

CHANNELS = 384
FRAMES = 4
COLS = 128
ROWS = 8
SEGMENTS = 2


def shard_levels(key, dims, split, least, top_value):
    factor_of, own = 1.0, jax.random.fold_in(key, 6)
    for dim, blocks in split:
        heights = jnp.exp(jax.random.uniform(jax.random.fold_in(own, dim), (blocks,), jnp.float32, least / len(split), top_value / len(split)))
        factor_of = factor_of * jnp.repeat(heights, dims[dim] // blocks).reshape([-1 if axis == dim else 1 for axis in range(len(dims))])
    return factor_of


def bell_draw(key, dims, scale, bound, pieces=(), dtype=jnp.bfloat16):
    values = scale * jax.random.normal(key, dims, jnp.float32)
    if pieces:
        values = values * shard_levels(key, dims, pieces, -0.22, 0.18)
    return jnp.clip(values, -bound, bound).astype(dtype)


def setup_inputs(seed: int = 0) -> dict:
    streams_of = jax.random.split(jax.random.key(seed), 6)
    features = bell_draw(streams_of[0], (FRAMES, ROWS, CHANNELS, COLS), 1.0, 6.0, ((1, 8), (2, 2)))
    caches = bell_draw(streams_of[1], (SEGMENTS, 2, 2, ROWS, CHANNELS, COLS), 0.7, 4.0, ((0, 2), (3, 8), (4, 2)))
    conv_weights = bell_draw(streams_of[2], (SEGMENTS, 2, CHANNELS, 3, 3, 3, CHANNELS), (27 * CHANNELS) ** -0.5, 0.0625, ((0, 2), (2, 2)))
    conv_bias = bell_draw(streams_of[3], (SEGMENTS, 2, CHANNELS), 0.5, 3.0, ((0, 2),), jnp.float32)
    norm_gain = jnp.clip(1.0 + 0.15 * jax.random.normal(streams_of[4], (SEGMENTS, 2, CHANNELS), jnp.float32), 0.25, 1.75)
    return {"features": features, "caches": caches, "conv_weights": conv_weights, "conv_bias": conv_bias, "norm_gain": norm_gain}


def normed_silu(source, gain):
    values = source.astype(jnp.float32)
    scale = lax.rsqrt(lax.optimization_barrier(jnp.mean(values * values, axis=2, keepdims=True)) + 1e-06)
    return jax.nn.silu(gain.astype(jnp.float32)[:, None] * values * scale).astype(jnp.bfloat16)

def causal_conv(window, kernel, offset):
    lhs = jnp.transpose(window.astype(jnp.float32), (0, 1, 3, 2))[None]
    rhs = jnp.transpose(kernel.astype(jnp.float32), (1, 2, 3, 4, 0))
    product = lax.conv_general_dilated(lhs, rhs, window_strides=(1, 1, 1), padding=((0, 0), (1, 1), (1, 1)), dimension_numbers=('NDHWC', 'DHWIO', 'NDHWC'), precision=lax.Precision.HIGHEST)[0]
    product = jnp.transpose(product, (0, 1, 3, 2))
    return product + offset.astype(jnp.float32)[:, None]

def reference(features, caches, conv_weights, conv_bias, norm_gain):
    block_input = features
    outputs = []
    cache_list = []
    for section in range(SEGMENTS):
        source = block_input
        kept = []
        for conv_index in range(2):
            activated = normed_silu(source, norm_gain[section, conv_index])
            window = jnp.concatenate([caches[section, conv_index], activated], axis=0)
            kept.append(window[-2:])
            product = causal_conv(window, conv_weights[section, conv_index], conv_bias[section, conv_index])
            if conv_index == 0:
                source = lax.optimization_barrier(product.astype(jnp.bfloat16))
            else:
                block_input = lax.optimization_barrier((block_input.astype(jnp.float32) + product).astype(jnp.bfloat16))
        outputs.append(block_input)
        cache_list.append(jnp.stack(kept))
    return (jnp.stack(outputs), jnp.stack(cache_list))
```

```python
import functools

import jax
import jax.numpy as jnp
from jax import lax
from jax.experimental import pallas as pl
from jax.experimental.pallas import tpu as pltpu
from jax.sharding import PartitionSpec as P

BF16 = jnp.bfloat16
F32 = jnp.float32
LANES = 128
VMEM_LIMIT = 56 * 1024 * 1024


def params():
    return pltpu.CompilerParams(vmem_limit_bytes=VMEM_LIMIT)


def turned(x, by):
    by = by % LANES
    return x if by == 0 else pltpu.roll(x, by, x.ndim - 1)


def lane_ids(shape):
    return lax.broadcasted_iota(jnp.int32, shape, len(shape) - 1)


def windows_kernel(count, halo, pitch, features_ref, caches_ref, sent_features_ref, sent_caches_ref):
    frames, channels, cols = features_ref.shape
    own = cols // count
    lane = lane_ids((channels, LANES))
    parts = [
        ([features_ref[f].astype(F32) for f in range(frames)], sent_features_ref),
        ([caches_ref[j, f].astype(F32) for j in range(2) for f in range(2)], sent_caches_ref),
    ]
    for values, sent_ref in parts:
        for device in range(count):
            first = own * device - halo
            total = jnp.zeros((channels, LANES), F32)
            for slot, value in enumerate(values):
                low = pitch * slot + max(0, -first)
                high = pitch * slot + min(pitch, cols - first)
                inside = jnp.logical_and(lane >= low, lane < high)
                total = jnp.where(inside, turned(value, pitch * slot - first), total)
            sent_ref[device] = total.astype(BF16)


def windows(features, caches, count, halo, pitch):
    channels = features.shape[1]
    shape = jax.ShapeDtypeStruct((count, channels, LANES), BF16)
    return pl.pallas_call(
        functools.partial(windows_kernel, count, halo, pitch),
        out_shape=(shape, shape),
        compiler_params=params(),
        name="windows",
    )(features, caches)


def activate(conv, pitch, cols, place_ref, source_ref, cache_ref, gain_ref, window_ref):
    rows, channels = source_ref.shape[1], source_ref.shape[2]
    lane = lane_ids((1, LANES))
    col = place_ref[0] + lane % pitch
    inside = jnp.logical_and(col >= 0, col < cols)
    zero_row = jnp.zeros((2 * channels, LANES), BF16)
    for tap in range(3):
        window_ref[tap, 0] = zero_row
        window_ref[tap, rows + 1] = zero_row

    def row_step(r, carry):
        halves = [source_ref[h, r].astype(F32) for h in range(2)]
        square = sum(jnp.sum(v * v, axis=0, keepdims=True) for v in halves)
        scale = lax.rsqrt(square / (2 * channels) + 1e-06)
        for h, value in enumerate(halves):
            at = pl.ds(h * channels, channels)
            v = gain_ref[at, :] * value * scale
            active = jnp.where(inside, v / (1.0 + jnp.exp(-v)), 0.0)
            active = active.astype(BF16).astype(F32)
            cached = cache_ref[h, r].astype(F32)
            window_ref[2, r + 1, at, :] = active.astype(BF16)
            one = jnp.where(lane < pitch, turned(cached, -pitch * (2 * conv + 1)), turned(active, pitch))
            window_ref[1, r + 1, at, :] = one.astype(BF16)
            two = jnp.where(lane < 2 * pitch, turned(cached, -pitch * 2 * conv), turned(active, 2 * pitch))
            window_ref[0, r + 1, at, :] = two.astype(BF16)
        return carry

    lax.fori_loop(0, rows, row_step, 0)


def conv_kernel(conv, halo, pitch, cols, own, place_ref, source_ref, cache_ref, gain_ref, bias_ref, kernel_ref, *rest):
    if conv == 0:
        out_ref, kept_ref, window_ref, weight_ref, sems = rest
    else:
        base_ref, kept_in_ref, older_ref, out_ref, pack_ref, window_ref, weight_ref, sems = rest
    rows, channels = source_ref.shape[1], source_ref.shape[2]
    taps = weight_ref.shape[0]
    copies = [
        pltpu.make_async_copy(kernel_ref.at[conv, t], weight_ref.at[t], sems.at[t]) for t in range(taps)
    ]
    for copy in copies:
        copy.start()
    activate(conv, pitch, cols, place_ref, source_ref, cache_ref, gain_ref, window_ref)
    for copy in copies:
        copy.wait()
    mine = pl.ds(pl.multiple_of(place_ref[1] * channels, channels), channels)
    lane = lane_ids((channels, LANES))

    def pair_step(p, carry):
        total = None
        for tap in range(taps):
            a, b = tap // 3, tap % 3
            block = jnp.concatenate([window_ref[a, 2 * p + b], window_ref[a, 2 * p + 1 + b]], axis=1)
            part = jnp.dot(weight_ref[tap], block, preferred_element_type=F32)
            total = part if total is None else total + part
        for k in range(2):
            r = 2 * p + k
            left, centre, right = [
                total[d * channels : (d + 1) * channels, k * LANES : (k + 1) * LANES] for d in range(3)
            ]
            product = turned(left, 1) + centre + turned(right, -1) + bias_ref[...]
            if conv == 0:
                out_ref[r] = product.astype(BF16)
                kept_ref[r] = window_ref[2, r + 1, mine, :]
            else:
                result = (base_ref[r].astype(F32) + product).astype(BF16)
                out_ref[r] = result
                values = result.astype(F32)
                firsts = kept_in_ref[r].astype(F32)
                seconds = window_ref[2, r + 1, mine, :].astype(F32)
                frames = LANES // pitch
                slots = [(values, f) for f in range(frames)]
                slots += [(firsts, frames - 2), (firsts, frames - 1), (seconds, frames - 2), (seconds, frames - 1)]
                packed = jnp.zeros((channels, LANES), F32)
                for slot, (value, f) in enumerate(slots):
                    here = jnp.logical_and(lane >= own * slot, lane < own * (slot + 1))
                    packed = jnp.where(here, turned(value, own * slot - pitch * f - halo), packed)
                keep = jnp.broadcast_to(place_ref[2] == 1, (channels, LANES))
                pack_ref[r] = jnp.where(keep, packed, older_ref[r].astype(F32)).astype(BF16)
        return carry

    lax.fori_loop(0, rows // 2, pair_step, 0)


def convolved(conv, halo, pitch, cols, own, place, source, cache, gain, bias, kernel, *more):
    rows, channels = source.shape[1], source.shape[2]
    taps, height, depth = kernel.shape[1:]
    shape = jax.ShapeDtypeStruct((rows, channels, LANES), BF16)
    vmem = pl.BlockSpec(memory_space=pltpu.VMEM)
    in_specs = [pl.BlockSpec(memory_space=pltpu.SMEM), vmem, vmem, vmem, vmem, pl.BlockSpec(memory_space=pl.ANY)]
    in_specs += [vmem] * len(more)
    return pl.pallas_call(
        functools.partial(conv_kernel, conv, halo, pitch, cols, own),
        out_shape=(shape, shape),
        in_specs=in_specs,
        out_specs=(vmem, vmem),
        scratch_shapes=[
            pltpu.VMEM((3, rows + 2, depth, LANES), BF16),
            pltpu.VMEM((taps, height, depth), BF16),
            pltpu.SemaphoreType.DMA((taps,)),
        ],
        compiler_params=params(),
        name=f"conv_{conv}",
    )(place, source, cache, gain, bias, kernel, *more)


def whole_rows_kernel(own, packed_ref, frames_ref, tails_ref):
    count, channels = packed_ref.shape[0], packed_ref.shape[1]
    lane = lane_ids((channels, LANES))
    frames = frames_ref.shape[0]
    for slot in range(frames + 4):
        total = jnp.zeros((channels, LANES), F32)
        for device in range(count):
            here = jnp.logical_and(lane >= own * device, lane < own * (device + 1))
            total = jnp.where(here, turned(packed_ref[device].astype(F32), own * (device - slot)), total)
        if slot < frames:
            frames_ref[slot] = total.astype(BF16)
        else:
            tails_ref[(slot - frames) // 2, (slot - frames) % 2] = total.astype(BF16)


def whole_rows(packed, own, frames):
    channels = packed.shape[1]
    return pl.pallas_call(
        functools.partial(whole_rows_kernel, own),
        out_shape=(
            jax.ShapeDtypeStruct((frames, channels, LANES), BF16),
            jax.ShapeDtypeStruct((2, 2, channels, LANES), BF16),
        ),
        compiler_params=params(),
        name="whole_rows",
    )(packed)


def shards(features, caches, conv_weights, conv_bias, norm_gain):
    count = lax.axis_size("rows")
    segments = lax.axis_size("segment")
    segment = lax.axis_index("segment")
    chan = lax.axis_index("chan")
    frames, _, channels, cols = features.shape
    own = cols // count
    halo = 2 * segments
    pitch = LANES // frames
    depth = conv_weights.shape[-1]
    kernels = jnp.transpose(conv_weights[0], (0, 2, 3, 4, 1, 5)).reshape(2, 9, 3 * channels, depth)
    biases = lax.dynamic_slice_in_dim(conv_bias[0], chan * channels, channels, 1)[:, :, None]
    gains = norm_gain[0][:, :, None]
    first = lax.axis_index("rows") * own - halo

    sent_features, sent_caches = windows(features[:, 0], caches[0][:, :, 0], count, halo, pitch)
    block_input = lax.all_to_all(sent_features, "rows", 0, 0, tiled=True)
    tails = lax.all_to_all(sent_caches, "rows", 0, 0, tiled=True)
    tails = lax.all_gather(tails, "chan", axis=0)
    packed = jnp.zeros_like(block_input)
    for period in range(segments):
        place = jnp.stack([first, chan, (segment == period).astype(jnp.int32)]).astype(jnp.int32)
        source = lax.all_gather(block_input, "chan", axis=0)
        middle, kept = convolved(
            0, halo, pitch, cols, own, place, source, tails, gains[0], biases[0], kernels
        )
        source = lax.all_gather(middle, "chan", axis=0)
        result, packed = convolved(
            1, halo, pitch, cols, own, place, source, tails, gains[1], biases[1], kernels, block_input, kept, packed
        )
        if period < segments - 1:
            pairs = [(i, (i + 1) % segments) for i in range(segments)]
            block_input = lax.ppermute(result, "segment", pairs)
    packed = lax.all_to_all(packed, "rows", 0, 0, tiled=True)
    section_out, tails_out = whole_rows(packed, own, frames)
    return (section_out[None, :, None], tails_out[None, :, :, None])


def solution(mesh):
    in_specs = (
        P(None, "rows", "chan", None),
        P("segment", None, None, "rows", "chan", None),
        P("segment", None, "chan", None, None, None, None),
        P("segment", None, None),
        P("segment", None, None),
    )
    out_specs = (
        P("segment", None, "rows", "chan", None),
        P("segment", None, None, "rows", "chan", None),
    )
    return jax.shard_map(shards, mesh=mesh, in_specs=in_specs, out_specs=out_specs, check_vma=False)
```

```python
import functools

import jax
import jax.numpy as jnp
from jax import lax
from jax.experimental import pallas as pl
from jax.experimental.pallas import tpu as pltpu
from jax.sharding import PartitionSpec as P

BF16 = jnp.bfloat16
F32 = jnp.float32
LANES = 128
SENT = 24
PITCH = 32
MIB = 1024 * 1024
VMEM = pl.BlockSpec(memory_space=pltpu.VMEM)
SMEM = pl.BlockSpec(memory_space=pltpu.SMEM)


def params(mib):
    return pltpu.CompilerParams(vmem_limit_bytes=mib * MIB)


def turned(x, by):
    by = by % LANES
    return x if by == 0 else pltpu.roll(x, by, x.ndim - 1)


def lanes_of(shape):
    return lax.broadcasted_iota(jnp.int32, shape, len(shape) - 1)


def between(lane, low, high):
    return jnp.logical_and(lane >= low, lane < high)


def tile(rows, channels, dtype=BF16):
    return jax.ShapeDtypeStruct((rows, channels, LANES), dtype)


def spread(x, lane):
    total = x
    for f in range(1, LANES // PITCH):
        total = jnp.where(between(lane, PITCH * f, PITCH * (f + 1)), turned(x, (PITCH - SENT) * f), total)
    return total


def gathered(x, lane):
    total = x
    for f in range(1, LANES // PITCH):
        total = jnp.where(between(lane, SENT * f, SENT * (f + 1)), turned(x, (SENT - PITCH) * f), total)
    return total


def fold(x, lane):
    whole = x.shape[0] * 3 // 4
    rest = x[whole:]
    tails = [turned(rest, 96 - 32 * i) for i in range(3)]
    return jnp.where(lane < 96, x[:whole], jnp.concatenate(tails, axis=0))


def unfold(x, lane):
    part = x.shape[0] // 3
    pieces = [turned(x[i * part : (i + 1) * part], 32 * i - 96) for i in range(3)]
    rest = jnp.where(lane < 32, pieces[0], jnp.where(lane < 64, pieces[1], pieces[2]))
    return jnp.concatenate([x, rest], axis=0)


def prepared_kernel(place_ref, gain_ref, bias_ref, gains_ref, biases_ref, all_ref):
    channels = biases_ref.shape[1]
    depth = gains_ref.shape[1]
    mine = pl.ds(pl.multiple_of(place_ref[1] * channels, channels), channels)
    for conv in range(2):
        for source, out in ((gain_ref, gains_ref.at[conv]), (bias_ref, all_ref)):
            for k in range(depth // LANES):
                at = slice(k * LANES, (k + 1) * LANES)
                out[at, :] = jnp.transpose(jnp.broadcast_to(source[conv : conv + 1, at], (LANES, LANES)))
        biases_ref[conv] = all_ref[mine, :]


def prepared(place, gain, bias, channels):
    depth = gain.shape[1]
    return pl.pallas_call(
        prepared_kernel,
        out_shape=(
            jax.ShapeDtypeStruct((2, depth, LANES), F32),
            jax.ShapeDtypeStruct((2, channels, LANES), F32),
        ),
        in_specs=[SMEM, VMEM, VMEM],
        out_specs=(VMEM, VMEM),
        scratch_shapes=[pltpu.VMEM((depth, LANES), F32)],
        compiler_params=params(8),
        name="prepared",
    )(place, gain, bias)


def windows_kernel(count, halo, features_ref, caches_ref, sent_ref):
    frames, channels, cols = features_ref.shape
    own = cols // count
    half = channels // 2
    lane = lanes_of((1, LANES))
    groups = [
        [features_ref[f] for f in range(frames)],
        [caches_ref[j, f] for j in range(2) for f in range(2)],
    ]
    for device in range(count):
        first = own * device - halo
        tiles = []
        for group in groups:
            total = jnp.zeros((channels, LANES), BF16)
            for slot, value in enumerate(group):
                low = SENT * slot + max(0, -first)
                high = SENT * slot + min(SENT, cols - first)
                total = jnp.where(between(lane, low, high), turned(value, SENT * slot - first), total)
            tiles.append(total)
        ahead, tails = tiles
        sent_ref[device, :channels] = jnp.where(lane < 96, ahead, turned(tails, 96))
        sent_ref[device, channels:] = jnp.where(lane < 64, turned(tails[:half], -32), turned(tails[half:], 32))


def windows(features, caches, count, halo):
    channels = features.shape[1]
    return pl.pallas_call(
        functools.partial(windows_kernel, count, halo),
        out_shape=tile(count, channels * 3 // 2),
        compiler_params=params(8 + count // 2),
        name="windows",
    )(features, caches)


def tails_of(sent, lane, channels):
    half = channels // 2
    extra = jnp.concatenate([turned(sent[channels:], 32), turned(sent[channels:], -32)], axis=0)
    return spread(jnp.where(lane < 32, turned(sent[:channels], -96), extra), lane)


def packed_row(own, halo, lane, result, kept):
    frames = LANES // PITCH
    slots = [(result, f) for f in range(frames)]
    slots += [(active, f) for active in kept for f in (frames - 2, frames - 1)]
    total = jnp.zeros(result.shape, BF16)
    for slot, (value, f) in enumerate(slots):
        here = between(lane, own * slot, own * (slot + 1))
        total = jnp.where(here, turned(value, own * slot - PITCH * f - halo), total)
    return total


def pack_kernel(period, own, halo, place_ref, result_ref, kept_0_ref, kept_1_ref, *rest):
    lane = lanes_of((1, LANES))
    out_ref = rest[-1]

    def step(r, carry):
        row = packed_row(own, halo, lane, result_ref[r], (kept_0_ref[r], kept_1_ref[r]))
        out_ref[r] = row if period == 0 else jnp.where(place_ref[2] == period, row, rest[0][r])
        return carry

    for_rows(result_ref.shape[0], step)


def for_rows(count, step):
    if count <= 8:
        for r in range(count):
            step(r, 0)
    else:
        lax.fori_loop(0, count, step, 0)


def packed_period(period, own, halo, place, result, kept, older):
    rows, channels = result.shape[:2]
    more = [] if older is None else [older]
    return pl.pallas_call(
        functools.partial(pack_kernel, period, own, halo),
        out_shape=tile(rows, channels),
        in_specs=[SMEM] + [VMEM] * (3 + len(more)),
        out_specs=VMEM,
        compiler_params=params(8 + rows // 2),
        name="packed_period",
    )(place, result, *kept, *more)


def conv_kernel(conv, first, last, halo, cols, own_cols, names, *refs):
    ref = dict(zip(names, refs))
    place_ref, weight_ref, window_ref = ref["place"], ref["weight"], ref["window"]
    own_ref, other_ref, kept_ref = ref["own"], ref["other"], ref["kept"]
    rows = own_ref.shape[0]
    taps, height, depth = weight_ref.shape
    channels = height // 3
    mine_first = place_ref[1] == 0
    lane = lanes_of((1, LANES))
    col = place_ref[0] + lane % PITCH
    inside = between(col, 0, cols)

    def ordered(own, other):
        return [jnp.where(mine_first, own, other), jnp.where(mine_first, other, own)]

    empty = jnp.zeros((depth, LANES), BF16)
    for tap in range(3):
        window_ref[tap, 0] = empty
        window_ref[tap, rows + 1] = empty

    def activate(r, carry):
        own, other = own_ref[r], other_ref[r]
        if conv == 0:
            if first:
                tails = ordered(*[tails_of(x, lane, channels) for x in (own, other)])
                own, other = [spread(x[:channels], lane) for x in (own, other)]
            else:
                own, other = [spread(unfold(x, lane), lane) for x in (own, other)]
            ref["base_out"][r] = own
        values = [x.astype(F32) for x in ordered(own, other)]
        square = sum(jnp.sum(v * v, axis=0, keepdims=True) for v in values)
        scale = jnp.where(inside, 0.5 * lax.rsqrt(square / depth + 1e-06), 0.0)
        kept = []
        for h, value in enumerate(values):
            at = slice(h * channels, (h + 1) * channels)
            t = ref["gains"][conv, at, :] * value * scale
            active = (t + t * jnp.tanh(t)).astype(BF16)
            if first and conv == 0:
                cached = tails[h]
                ref["tails_out"][r, at, :] = cached
            else:
                cached = ref["tails"][r, at, :]
            window_ref[2, r + 1, at, :] = active
            window_ref[1, r + 1, at, :] = jnp.where(
                lane < PITCH, turned(cached, -PITCH * (2 * conv + 1)), turned(active, PITCH)
            )
            window_ref[0, r + 1, at, :] = jnp.where(
                lane < 2 * PITCH, turned(cached, -PITCH * 2 * conv), turned(active, 2 * PITCH)
            )
            kept.append(active)
        kept_ref[r] = jnp.where(mine_first, *kept)
        return carry

    def multiply(r0, count):
        block = jnp.concatenate(
            [
                jnp.concatenate([window_ref[t // 3, r0 + t % 3 + i] for i in range(count)], axis=1)
                for t in range(taps)
            ],
            axis=0,
        )
        weight = jnp.concatenate([weight_ref[t] for t in range(taps)], axis=1)
        total = jnp.dot(weight, block, preferred_element_type=F32)
        offset = ref["biases"][conv]
        for k in range(count):
            r = r0 + k
            left, centre, right = [
                total[d * channels : (d + 1) * channels, k * LANES : (k + 1) * LANES] for d in range(3)
            ]
            product = turned(left, 1) + centre + turned(right, -1) + offset
            if conv == 0:
                ref["out"][r] = product.astype(BF16)
                continue
            result = (ref["base"][r].astype(F32) + product).astype(BF16)
            if last:
                row = packed_row(own_cols, halo, lane, result, (ref["kept_0"][r], kept_ref[r]))
                ref["out"][r] = jnp.where(place_ref[2] == last, row, ref["older"][r])
            else:
                ref["out"][r] = result
                ref["sent"][r] = fold(gathered(result, lane), lane)

    steps = 4
    if rows <= 8:
        done = 0
        for r0 in range(0, rows, steps):
            need = min(rows, r0 + steps + 1)
            for r in range(done, need):
                activate(r, 0)
            done = need
            multiply(r0, steps)
    else:
        lax.fori_loop(0, rows, activate, 0)
        lax.fori_loop(0, rows // steps, lambda g, c: (multiply(g * steps, steps), c)[1], 0)


def convolved(conv, first, last, halo, cols, own_cols, arrays, outs):
    rows = arrays["own"].shape[0]
    taps, height, depth = arrays["weight"].shape
    scratch = {"window": pltpu.VMEM((3, rows + 2, depth, LANES), BF16)}
    if "kept" not in outs:
        scratch["kept"] = pltpu.VMEM((rows, height // 3, LANES), BF16)
    names = [*arrays, *outs, *scratch]
    results = pl.pallas_call(
        functools.partial(conv_kernel, conv, first, last, halo, cols, own_cols, names),
        out_shape=[tile(rows, size) for size in outs.values()],
        in_specs=[SMEM if name == "place" else VMEM for name in arrays],
        out_specs=[VMEM] * len(outs),
        scratch_shapes=list(scratch.values()),
        compiler_params=params(9 + 5 * rows // 8),
        name=f"conv_{conv}",
    )(*arrays.values())
    return dict(zip(outs, results))


def whole_rows_kernel(own, packed_ref, frames_ref, tails_ref):
    count, channels = packed_ref.shape[0], packed_ref.shape[1]
    lane = lanes_of((1, LANES))
    frames = frames_ref.shape[0]
    for slot in range(frames + 4):
        total = jnp.zeros((channels, LANES), BF16)
        for device in range(count):
            here = between(lane, own * device, own * (device + 1))
            total = jnp.where(here, turned(packed_ref[device], own * (device - slot)), total)
        if slot < frames:
            frames_ref[slot] = total
        else:
            tails_ref[(slot - frames) // 2, (slot - frames) % 2] = total


def whole_rows(packed, own, frames):
    count, channels = packed.shape[:2]
    return pl.pallas_call(
        functools.partial(whole_rows_kernel, own),
        out_shape=(tile(frames, channels), jax.ShapeDtypeStruct((2, 2, channels, LANES), BF16)),
        compiler_params=params(8 + count // 2),
        name="whole_rows",
    )(packed)


def swapped(x):
    return lax.ppermute(x, "chan", [(0, 1), (1, 0)])


def shards(features, caches, conv_weights, conv_bias, norm_gain):
    count = lax.axis_size("rows")
    segments = lax.axis_size("segment")
    frames, _, channels, cols = features.shape
    depth = conv_weights.shape[-1]
    own = cols // count
    halo = 2 * segments
    assert own + 2 * halo <= SENT and frames * PITCH == LANES
    kernels = jnp.transpose(conv_weights[0], (0, 2, 3, 4, 1, 5)).reshape(2, 9, 3 * channels, depth)
    first = lax.axis_index("rows") * own - halo
    place = jnp.stack([first, lax.axis_index("chan"), lax.axis_index("segment")]).astype(jnp.int32)

    sent = windows(features[:, 0], caches[0][:, :, 0], count, halo)
    gains, biases = prepared(place, norm_gain[0], conv_bias[0], channels)
    source = lax.all_to_all(sent, "rows", 0, 0, tiled=True)
    source, gains, biases = lax.optimization_barrier((source, gains, biases))
    common = {"place": place, "gains": gains, "biases": biases}
    packed = tails = None
    kernels_0 = kernels[0]
    for period in range(segments):
        last = period if period == segments - 1 else 0
        arrays = common | {"weight": kernels_0, "own": source, "other": swapped(source)}
        outs = {"out": channels, "kept": channels, "base_out": channels}
        if period == 0:
            outs["tails_out"] = depth
        else:
            arrays["tails"] = tails
        one = convolved(0, period == 0, last, halo, cols, own, arrays, outs)
        middle = one["out"]
        if period == 0:
            tails = one["tails_out"]
            middle, kernels = lax.optimization_barrier((middle, kernels))
            kernels_1 = kernels[1]
        arrays = common | {"weight": kernels_1, "own": middle, "other": swapped(middle)}
        arrays |= {"tails": tails, "base": one["base_out"]}
        if last:
            arrays |= {"kept_0": one["kept"], "older": packed}
            packed = convolved(1, False, last, halo, cols, own, arrays, {"out": channels})["out"]
        else:
            outs = {"out": channels, "kept": channels, "sent": channels * 3 // 4}
            two = convolved(1, False, last, halo, cols, own, arrays, outs)
            source = lax.ppermute(two["sent"], "segment", [(i, (i + 1) % segments) for i in range(segments)])
            kept = (one["kept"], two["kept"])
            packed = packed_period(period, own, halo, place, two["out"], kept, packed)
    packed = lax.all_to_all(packed, "rows", 0, 0, tiled=True)
    section_out, tails_out = whole_rows(packed, own, frames)
    return (section_out[None, :, None], tails_out[None, :, :, None])


def solution(mesh):
    in_specs = (
        P(None, "rows", "chan", None),
        P("segment", None, None, "rows", "chan", None),
        P("segment", None, "chan", None, None, None, None),
        P("segment", None, None),
        P("segment", None, None),
    )
    out_specs = (
        P("segment", None, "rows", "chan", None),
        P("segment", None, None, "rows", "chan", None),
    )
    return jax.shard_map(shards, mesh=mesh, in_specs=in_specs, out_specs=out_specs, check_vma=False)
```

```python
import functools

import jax
import jax.numpy as jnp
from jax import lax
from jax.experimental import pallas as pl
from jax.experimental.pallas import tpu as pltpu
from jax.sharding import PartitionSpec as P

BF16 = jnp.bfloat16
F32 = jnp.float32
LANES = 128
MIB = 1024 * 1024
VMEM = pl.BlockSpec(memory_space=pltpu.VMEM)
SMEM = pl.BlockSpec(memory_space=pltpu.SMEM)
TAILS = 4


def params(mib):
    return pltpu.CompilerParams(vmem_limit_bytes=mib * MIB)


def turned(x, by):
    by = by % LANES
    return x if by == 0 else pltpu.roll(x, by, x.ndim - 1)


def tiles(count, channels, dtype=BF16):
    return jax.ShapeDtypeStruct((count, channels, LANES), dtype)


def prepared_kernel(place_ref, gain_ref, bias_ref, kernels_ref, gains_ref, biases_ref, all_ref):
    channels = biases_ref.shape[1]
    depth = gains_ref.shape[1]
    mine = pl.ds(pl.multiple_of(place_ref[0] * channels, channels), channels)
    for conv in range(2):
        for source, out in ((gain_ref, gains_ref.at[conv]), (bias_ref, all_ref)):
            for k in range(depth // LANES):
                at = slice(k * LANES, (k + 1) * LANES)
                out[at, :] = jnp.transpose(jnp.broadcast_to(source[conv : conv + 1, at], (LANES, LANES)))
        biases_ref[conv] = all_ref[mine, :]


def prepared(place, gain, bias, kernels, channels):
    depth = gain.shape[1]
    return pl.pallas_call(
        prepared_kernel,
        out_shape=(
            jax.ShapeDtypeStruct((2, depth, LANES), F32),
            jax.ShapeDtypeStruct((2, channels, LANES), F32),
        ),
        in_specs=[SMEM, VMEM, VMEM, VMEM],
        out_specs=(VMEM, VMEM),
        scratch_shapes=[pltpu.VMEM((depth, LANES), F32)],
        compiler_params=params(16),
        name="prepared",
    )(place, gain, bias, kernels)


class Part:
    def __init__(self, conv, ref, count):
        self.conv, self.ref, self.count = conv, ref, count
        self.window = ref["window"]
        self.weight = ref["weight"]
        _, self.taps, height, self.depth = self.weight.shape
        self.channels = height // 3
        self.mine_first = ref["place"][0] == 0
        self.side = ref["place"][1]
        self.lane = lax.broadcasted_iota(jnp.int32, (1, LANES), 1)

    def ordered(self, name, tile):
        own, other = self.ref[name][tile], self.ref[name + "_other"][tile]
        return [jnp.where(self.mine_first, own, other), jnp.where(self.mine_first, other, own)]

    def activate(self, slot, frame, name, tile, valid=None):
        values = [x.astype(F32) for x in self.ordered(name, tile)]
        square = sum(jnp.sum(v * v, axis=0, keepdims=True) for v in values)
        scale = 0.5 * lax.rsqrt(square / self.depth + 1e-06)
        if valid is not None:
            scale = jnp.where(valid, scale, 0.0)
        kept = []
        for h, value in enumerate(values):
            at = slice(h * self.channels, (h + 1) * self.channels)
            t = self.ref["gains"][self.conv, at, :] * value * scale
            active = (t + t * jnp.tanh(t)).astype(BF16)
            self.window[slot, frame + 2, at, :] = active
            kept.append(active)
        return jnp.where(self.mine_first, *kept)

    def cached(self, slot, name, tile):
        for f in range(2):
            for h, value in enumerate(self.ordered(name, tile + 2 * self.conv + f)):
                self.window[slot, f, h * self.channels : (h + 1) * self.channels, :] = value

    def product(self, slots, first, frames):
        block, weight = [], []
        for slot, tap in slots:
            row_tap = 1 + self.side * (tap - 1)
            for a in range(3):
                weight.append(self.weight[self.conv, 3 * a + row_tap])
                block.append(
                    jnp.concatenate([self.window[slot, first + f + a] for f in range(frames)], axis=1)
                )
        total = jnp.dot(
            jnp.concatenate(weight, axis=1), jnp.concatenate(block, axis=0), preferred_element_type=F32
        )
        sums = []
        for f in range(frames):
            left, centre, right = [
                total[d * self.channels : (d + 1) * self.channels, f * LANES : (f + 1) * LANES] for d in range(3)
            ]
            left = jnp.where(self.lane == 0, 0.0, turned(left, 1))
            right = jnp.where(self.lane == LANES - 1, 0.0, turned(right, -1))
            sums.append(left + centre + right)
        return sums


def near_kernel(frames, base, names, *refs):
    ref = dict(zip(names, refs))
    part = Part(0, ref, frames)
    sums = ref["sums"]
    bias = ref["biases"][0]
    places = [("own", 0), ("beside", 0), ("beside", 1), ("beside", 2)]
    cache_tiles = ref["tails_own"].shape[0]

    def load(slot):
        name, group = places[slot]
        part.cached(slot, "tails_" + name, group * cache_tiles)
        for f in range(frames):
            kept = part.activate(slot, f, name, group * (frames + base) + base + f)
            if slot == 0 and f >= frames - 2:
                ref["kept"][f - frames + 2] = kept

    def store(o, slots):
        for f, value in enumerate(part.product(slots, 0, frames)):
            sums[(o + 1) * frames + f] = value + bias

    load(0)
    load(1)
    store(0, [(1, 0), (0, 1)])
    load(2)
    store(-1, [(2, 0), (1, 1), (0, 2)])
    load(3)
    store(1, [(0, 0), (3, 2)])


def far_kernel(frames, base, names, *refs):
    ref = dict(zip(names, refs))
    part = Part(0, ref, frames)
    out, sums = ref["out"], ref["sums"]
    part.cached(0, "tails_diagonal", 0)
    for f in range(frames):
        part.activate(0, f, "diagonal", base + f)
    for f in range(frames):
        out[f] = sums[f].astype(BF16)
    for o, tap in ((0, 2), (1, 1)):
        for f, value in enumerate(part.product([(0, tap)], 0, frames)):
            at = (o + 1) * frames + f
            out[at] = (sums[at] + value).astype(BF16)


def second_kernel(frames, base, period, count, names, *refs):
    ref = dict(zip(names, refs))
    part = Part(1, ref, frames)
    row, segment = ref["place"][2], ref["place"][3]
    bias = ref["biases"][1]
    places = [("tails_own", 0), ("tails_beside", 0), ("tails_diagonal", 0)]
    offsets = (0, -1, 1)

    def load(first, last):
        for slot, q in enumerate(offsets):
            at = row + part.side * q
            valid = None if q == 0 else jnp.broadcast_to(jnp.logical_and(at >= 0, at < count), (1, LANES))
            for f in range(first, last):
                kept = part.activate(slot, f, "middle", (q + 1) * frames + f, valid)
                if slot == 0 and f >= frames - 2:
                    new_tails[2 + f - frames + 2] = kept

    new_tails = {f: ref["kept"][f] for f in range(2)}

    def store(first, last):
        sums = part.product([(1, 0), (0, 1), (2, 2)], first, last - first)
        for f, value in enumerate(sums, first):
            result = (ref["source"][base + f].astype(F32) + (value + bias)).astype(BF16)
            if "result" in ref:
                ref["result"][f] = result
            ref["out"][f] = jnp.where(segment == period, result, ref["older"][f]) if period else result

    for slot, (name, tile) in enumerate(places):
        part.cached(slot, name, tile)
    half = frames // 2
    load(0, half)
    store(0, half)
    load(half, frames)
    store(half, frames)
    for f in range(4):
        tail = new_tails[f]
        ref["tails"][f] = jnp.where(segment == period, tail, ref["older_tails"][f]) if period else tail


def call(kernel, name, arrays, outs, slots):
    depth = arrays["weight"].shape[-1]
    frames = 4
    scratch = {"window": pltpu.VMEM((slots, frames + 2, depth, LANES), BF16)}
    names = [*arrays, *outs, *scratch]
    results = pl.pallas_call(
        functools.partial(kernel, names),
        out_shape=list(outs.values()),
        in_specs=[SMEM if key == "place" else VMEM for key in arrays],
        out_specs=[VMEM] * len(outs),
        scratch_shapes=list(scratch.values()),
        compiler_params=params(16),
        name=name,
    )(*arrays.values())
    return dict(zip(outs, results))


def swapped(x):
    return lax.ppermute(x, "chan", [(0, 1), (1, 0)])


def with_other(name, x):
    return {name: x, name + "_other": swapped(x)}


def exchanged(x, count, kind, pair, *beside_it):
    pairs = count // 2
    across = [(i, i ^ 1) for i in range(count)]
    even, odd = [], []
    for i in range(count):
        k = i // 2
        for k_to, group in ((k ^ 1, even), (k + 1 if k % 2 else k - 1, odd)):
            if 0 <= k_to < pairs:
                group.append((i, 2 * k_to + i % 2))
    beside = lax.ppermute(x, "rows", across)
    a = lax.ppermute(x, "rows", even)
    b = lax.ppermute(x, "rows", odd)
    if beside_it:
        beside, a, b, beside_it = lax.optimization_barrier((beside, a, b, beside_it))
    to_a = kind == pair % 2
    near, far = jnp.where(to_a, a, b), jnp.where(to_a, b, a)
    diagonal = lax.ppermute(near, "rows", across)
    return jnp.concatenate([beside, near, far], axis=0), diagonal, beside_it


def shards(features, caches, conv_weights, conv_bias, norm_gain):
    count = lax.axis_size("rows")
    segments = lax.axis_size("segment")
    row = lax.axis_index("rows")
    frames, _, channels, _ = features.shape
    depth = conv_weights.shape[-1]
    kernels = jnp.transpose(conv_weights[0], (0, 2, 3, 4, 1, 5)).reshape(2, 9, 3 * channels, depth)
    kind, pair = row % 2, row // 2
    place = [lax.axis_index("chan"), 2 * kind - 1, row, lax.axis_index("segment")]
    place = jnp.stack(place).astype(jnp.int32)

    source = jnp.concatenate([caches[0].reshape(TAILS, channels, LANES), features[:, 0]], axis=0)
    fixed = prepared(place, norm_gain[0], conv_bias[0], kernels, channels)
    out = tails = None
    cached = {}
    for period in range(segments):
        base = TAILS if period == 0 else 0
        own = with_other("own", source)
        beside, diagonal, done = exchanged(source, count, kind, pair, *(() if period else fixed))
        beside = with_other("beside", beside)
        if period == 0:
            common = {"place": place, "gains": done[0], "biases": done[1], "weight": kernels}
            cached = {"tails_" + key: value for key, value in (own | beside).items()}
        tails_of = lambda *keys: {"tails_" + k + o: cached["tails_" + k + o] for k in keys for o in ("", "_other")}
        outs = {"sums": tiles(3 * frames, channels, F32), "kept": tiles(2, channels)}
        near = call(
            functools.partial(near_kernel, frames, base),
            "near_rows",
            common | own | beside | tails_of("own", "beside"),
            outs,
            4,
        )
        diagonal, sums = lax.optimization_barrier((diagonal, near["sums"]))
        diagonal = with_other("diagonal", diagonal)
        if period == 0:
            cached |= {"tails_" + key: value for key, value in diagonal.items()}
        middle = call(
            functools.partial(far_kernel, frames, base),
            "far_row",
            common | diagonal | tails_of("diagonal") | {"sums": sums},
            {"out": tiles(3 * frames, channels)},
            1,
        )["out"]
        arrays = common | with_other("middle", middle) | tails_of("own", "beside", "diagonal")
        arrays |= {"source": source, "kept": near["kept"]}
        outs = {"out": tiles(frames, channels), "tails": tiles(TAILS, channels)}
        if period:
            arrays |= {"older": out, "older_tails": tails}
            if period < segments - 1:
                outs["result"] = tiles(frames, channels)
        second = call(
            functools.partial(second_kernel, frames, base, period, count), "second", arrays, outs, 3
        )
        out, tails = second["out"], second["tails"]
        if period < segments - 1:
            result = second["result"] if period else out
            source = lax.ppermute(result, "segment", [(i, (i + 1) % segments) for i in range(segments)])
    return (out[None, :, None], tails.reshape(1, 2, 2, 1, channels, LANES))


def solution(mesh):
    in_specs = (
        P(None, "rows", "chan", None),
        P("segment", None, None, "rows", "chan", None),
        P("segment", None, "chan", None, None, None, None),
        P("segment", None, None),
        P("segment", None, None),
    )
    out_specs = (
        P("segment", None, "rows", "chan", None),
        P("segment", None, None, "rows", "chan", None),
    )
    return jax.shard_map(shards, mesh=mesh, in_specs=in_specs, out_specs=out_specs, check_vma=False)
```

```python
import functools

import jax
import jax.numpy as jnp
from jax import lax
from jax.experimental import pallas as pl
from jax.experimental.pallas import tpu as pltpu
from jax.sharding import PartitionSpec as P

BF16 = jnp.bfloat16
F32 = jnp.float32
LANES = 128
MIB = 1024 * 1024
VMEM = pl.BlockSpec(memory_space=pltpu.VMEM)
SMEM = pl.BlockSpec(memory_space=pltpu.SMEM)
TAILS = 2


def params(mib):
    return pltpu.CompilerParams(vmem_limit_bytes=mib * MIB)


def turned(x, by):
    by = by % LANES
    return x if by == 0 else pltpu.roll(x, by, x.ndim - 1)


def tiles(count, channels, dtype=BF16):
    return jax.ShapeDtypeStruct((count, channels, LANES), dtype)


def prepared_kernel(place_ref, gain_ref, bias_ref, kernels_ref, gains_ref, biases_ref, all_ref):
    channels = biases_ref.shape[1]
    depth = gains_ref.shape[1]
    mine = pl.ds(pl.multiple_of(place_ref[0] * channels, channels), channels)
    for conv in range(2):
        for source, out in ((gain_ref, gains_ref.at[conv]), (bias_ref, all_ref)):
            for k in range(depth // LANES):
                at = slice(k * LANES, (k + 1) * LANES)
                out[at, :] = jnp.transpose(jnp.broadcast_to(source[conv : conv + 1, at], (LANES, LANES)))
        biases_ref[conv] = all_ref[mine, :]


def prepared(place, gain, bias, kernels, channels):
    depth = gain.shape[1]
    return pl.pallas_call(
        prepared_kernel,
        out_shape=(
            jax.ShapeDtypeStruct((2, depth, LANES), F32),
            jax.ShapeDtypeStruct((2, channels, LANES), F32),
        ),
        in_specs=[SMEM, VMEM, VMEM, VMEM],
        out_specs=(VMEM, VMEM),
        scratch_shapes=[pltpu.VMEM((depth, LANES), F32)],
        compiler_params=params(16),
        name="prepared",
    )(place, gain, bias, kernels)


class Part:
    def __init__(self, conv, ref):
        self.conv, self.ref = conv, ref
        self.window = ref["window"]
        self.weight = ref["weight"]
        _, self.taps, height, self.depth = self.weight.shape
        self.channels = height // 3
        self.mine_first = ref["place"][0] == 0
        self.side = ref["place"][1]
        self.lane = lax.broadcasted_iota(jnp.int32, (1, LANES), 1)

    def ordered(self, name, tile):
        own, other = self.ref[name][tile], self.ref[name + "_other"][tile]
        return [jnp.where(self.mine_first, own, other), jnp.where(self.mine_first, other, own)]

    def activate(self, slot, frame, name, tile, valid=None):
        values = [x.astype(F32) for x in self.ordered(name, tile)]
        square = sum(jnp.sum(v * v, axis=0, keepdims=True) for v in values)
        scale = 0.5 * lax.rsqrt(square / self.depth + 1e-06)
        if valid is not None:
            scale = jnp.where(valid, scale, 0.0)
        kept = []
        for h, value in enumerate(values):
            at = slice(h * self.channels, (h + 1) * self.channels)
            t = self.ref["gains"][self.conv, at, :] * value * scale
            active = (t + t * jnp.tanh(t)).astype(BF16)
            self.window[slot, frame + 2, at, :] = active
            kept.append(active)
        return jnp.where(self.mine_first, *kept)

    def cached(self, slot, name, tile):
        for f in range(2):
            for h, value in enumerate(self.ordered(name, tile + f)):
                self.window[slot, f, h * self.channels : (h + 1) * self.channels, :] = value

    def product(self, slots, first, frames, held=(True, True)):
        block, weight = [], []
        nothing = jnp.zeros((self.depth, LANES), BF16)
        for slot, tap in slots:
            row_tap = 1 + self.side * (tap - 1)
            for a in range(3):
                wanted = [first + f + a for f in range(frames)]
                here = [held[0 if frame < 2 else 1] for frame in wanted]
                if any(here):
                    tile = [self.window[slot, frame] if h else nothing for frame, h in zip(wanted, here)]
                    weight.append(self.weight[self.conv, 3 * a + row_tap])
                    block.append(jnp.concatenate(tile, axis=1))
        total = jnp.dot(
            jnp.concatenate(weight, axis=1), jnp.concatenate(block, axis=0), preferred_element_type=F32
        )
        sums = []
        for f in range(frames):
            left, centre, right = [
                total[d * self.channels : (d + 1) * self.channels, f * LANES : (f + 1) * LANES] for d in range(3)
            ]
            left = jnp.where(self.lane == 0, 0.0, turned(left, 1))
            right = jnp.where(self.lane == LANES - 1, 0.0, turned(right, -1))
            sums.append(left + centre + right)
        return sums


def near_kernel(frames, base, names, *refs):
    ref = dict(zip(names, refs))
    part = Part(0, ref)
    half = frames // 2
    bias = ref["biases"][0]
    places = [("own", 0), ("beside", 0), ("beside", 1), ("beside", 2)]

    def load(slot, first):
        name, group = places[slot]
        if first == 0:
            part.cached(slot, "tails_" + name, group * ref["tails_own"].shape[0])
        for f in range(first, first + half):
            kept = part.activate(slot, f, name, group * (frames + base) + base + f)
            if slot == 0 and f >= frames - 2:
                ref["kept"][f - frames + 2] = kept

    def store(q, slots, first):
        for f, value in enumerate(part.product(slots, first, half), first):
            ref["sums"][(q + 1) * frames + f] = value + bias

    for first in (0, half):
        load(0, first)
        load(1, first)
        store(0, [(1, 0), (0, 1)], first)
        load(2, first)
        store(-1, [(2, 0), (1, 1), (0, 2)], first)
        load(3, first)
        store(1, [(0, 0), (3, 2)], first)


def cached_kernel(names, *refs):
    ref = dict(zip(names, refs))
    first, second = Part(0, ref), Part(1, ref)
    tails = ref["tails_own"].shape[0]
    held = (True, False)
    first.cached(0, "tails_own", 0)
    for group in range(3):
        first.cached(1 + group, "tails_beside", group * tails)
    first.cached(4, "tails_diagonal", 0)
    for q, slots in ((-1, [(2, 0), (1, 1), (0, 2)]), (0, [(1, 0), (0, 1), (4, 2)]), (1, [(0, 0), (4, 1), (3, 2)])):
        for f, value in enumerate(first.product(slots, 0, 2, held)):
            ref["cached_sums"][2 * (q + 1) + f] = value + ref["biases"][0]
    for slot in range(3):
        second.cached(5 + slot, "seconds", TAILS * slot)
    for f, value in enumerate(second.product([(6, 0), (5, 1), (7, 2)], 0, 2, held)):
        ref["cached_seconds"][f] = value + ref["biases"][1]


def own_kernel(frames, names, *refs):
    ref = dict(zip(names, refs))
    part = Part(0, ref)
    half = frames // 2
    for first in (0, half):
        for f in range(first, first + half):
            kept = part.activate(0, f, "own", f)
            if f >= frames - 2:
                ref["kept"][f - frames + 2] = kept
        for q in (-1, 0, 1):
            for f, value in enumerate(part.product([(0, 1 - q)], first, half, (False, True)), first):
                before = ref["cached_sums"][2 * (q + 1) + f] if f < 2 else ref["biases"][0]
                ref["sums"][(q + 1) * frames + f] = value + before


def beside_kernel(frames, names, *refs):
    ref = dict(zip(names, refs))
    part = Part(0, ref)
    half = frames // 2

    def load(slot, first):
        for f in range(first, first + half):
            part.activate(slot, f, "beside", slot * frames + f)

    def store(q, slots, first):
        for f, value in enumerate(part.product(slots, first, half, (False, True)), first):
            at = (q + 1) * frames + f
            ref["sums"][at] = ref["sums_before"][at] + value

    for first in (0, half):
        load(0, first)
        store(0, [(0, 0)], first)
        load(1, first)
        store(-1, [(1, 0), (0, 1)], first)
        load(2, first)
        store(1, [(2, 2)], first)


def far_kernel(frames, base, names, *refs):
    ref = dict(zip(names, refs))
    part = Part(0, ref)
    half = frames // 2
    out, sums = ref["out"], ref["sums"]
    if base:
        part.cached(0, "tails_diagonal", 0)
    for first in (0, half):
        for f in range(first, first + half):
            part.activate(0, f, "diagonal", base + f)
            out[f] = sums[f].astype(BF16)
        for q, tap in ((0, 2), (1, 1)):
            for f, value in enumerate(part.product([(0, tap)], first, half, (base > 0, True)), first):
                at = (q + 1) * frames + f
                out[at] = (sums[at] + value).astype(BF16)


def second_kernel(frames, base, period, count, names, *refs):
    ref = dict(zip(names, refs))
    part = Part(1, ref)
    row, segment = ref["place"][2], ref["place"][3]
    bias = ref["biases"][1]
    offsets = (0, -1, 1)

    def load(first, last):
        for slot, q in enumerate(offsets):
            at = row + part.side * q
            valid = None if q == 0 else jnp.broadcast_to(jnp.logical_and(at >= 0, at < count), (1, LANES))
            for f in range(first, last):
                kept = part.activate(slot, f, "middle", (q + 1) * frames + f, valid)
                if slot == 0 and f >= frames - 2:
                    new_tails[2 + f - frames + 2] = kept

    new_tails = {f: ref["kept"][f] for f in range(2)}

    def store(first, last):
        sums = part.product([(1, 0), (0, 1), (2, 2)], first, last - first, (period == 0, True))
        for f, value in enumerate(sums, first):
            before = ref["cached_seconds"][f] if period and f < 2 else bias
            result = (ref["source"][base + f].astype(F32) + (value + before)).astype(BF16)
            if "result" in ref:
                ref["result"][f] = result
            ref["out"][f] = jnp.where(segment == period, result, ref["older"][f]) if period else result

    if period == 0:
        for slot in range(len(offsets)):
            part.cached(slot, "seconds", TAILS * slot)
    half = frames // 2
    load(0, half)
    store(0, half)
    load(half, frames)
    store(half, frames)
    for f in range(4):
        tail = new_tails[f]
        ref["tails"][f] = jnp.where(segment == period, tail, ref["older_tails"][f]) if period else tail


def call(kernel, name, arrays, outs, slots):
    depth = arrays["weight"].shape[-1]
    frames = 4
    scratch = {"window": pltpu.VMEM((slots, frames + 2, depth, LANES), BF16)}
    names = [*arrays, *outs, *scratch]
    results = pl.pallas_call(
        functools.partial(kernel, names),
        out_shape=list(outs.values()),
        in_specs=[SMEM if key == "place" else VMEM for key in arrays],
        out_specs=[VMEM] * len(outs),
        scratch_shapes=list(scratch.values()),
        compiler_params=params(16),
        name=name,
    )(*arrays.values())
    return dict(zip(outs, results))


def swapped(x):
    return lax.ppermute(x, "chan", [(0, 1), (1, 0)])


def with_other(name, x):
    return {name: x, name + "_other": swapped(x)}


def across(count):
    return [(i, i ^ 1) for i in range(count)]


def exchanged(x, count):
    pairs = count // 2
    even, odd = [], []
    for i in range(count):
        k = i // 2
        for k_to, group in ((k ^ 1, even), (k + 1 if k % 2 else k - 1, odd)):
            if 0 <= k_to < pairs:
                group.append((i, 2 * k_to + i % 2))
    return [lax.ppermute(x, "rows", pairs) for pairs in (across(count), even, odd)]


def shards(features, caches, conv_weights, conv_bias, norm_gain):
    count = lax.axis_size("rows")
    segments = lax.axis_size("segment")
    row = lax.axis_index("rows")
    frames, _, channels, _ = features.shape
    depth = conv_weights.shape[-1]
    kernels = jnp.transpose(conv_weights[0], (0, 2, 3, 4, 1, 5)).reshape(2, 9, 3 * channels, depth)
    kind, pair = row % 2, row // 2
    place = [lax.axis_index("chan"), 2 * kind - 1, row, lax.axis_index("segment")]
    place = jnp.stack(place).astype(jnp.int32)

    source = jnp.concatenate([caches[0].reshape(2 * TAILS, channels, LANES), features[:, 0]], axis=0)
    gains, biases = prepared(place, norm_gain[0], conv_bias[0], kernels, channels)
    source = jnp.concatenate([caches[0].reshape(2 * TAILS, channels, LANES), features[:, 0]], axis=0)
    sums_shape, kept_shape = tiles(3 * frames, channels, F32), tiles(2, channels)
    near_first = kind == pair % 2
    out = tails = cached_seconds = None
    for period in range(segments):
        base = 0 if period else TAILS
        beside, even, odd = exchanged(source, count)
        if period == 0:
            beside, even, odd, gains, biases = lax.optimization_barrier((beside, even, odd, gains, biases))
            common = {"place": place, "gains": gains, "biases": biases, "weight": kernels}
        else:
            arrays = common | with_other("own", source) | {"cached_sums": cached_sums}
            outs = {"sums": sums_shape, "kept": kept_shape}
            first = call(functools.partial(own_kernel, frames), "own_row", arrays, outs, 1)
            sums, kept = first["sums"], first["kept"]
            even, odd, sums, kept = lax.optimization_barrier((even, odd, sums, kept))
        near, far = jnp.where(near_first, even, odd), jnp.where(near_first, odd, even)
        if period == 0:
            seconds = [x[TAILS : 2 * TAILS] for x in (source, beside, near)]
            source, beside, near, far = [
                jnp.concatenate([x[:TAILS], x[2 * TAILS :]], axis=0) for x in (source, beside, near, far)
            ]
        diagonal = lax.ppermute(near, "rows", across(count))
        arrays = with_other("beside", jnp.concatenate([beside, near, far], axis=0))
        if period == 0:
            arrays |= with_other("own", source)
            cached = {"tails_" + key: value for key, value in arrays.items()}
            outs = {"sums": sums_shape, "kept": kept_shape}
            first = call(functools.partial(near_kernel, frames, base), "near_rows", common | arrays | cached, outs, 4)
            sums, kept = first["sums"], first["kept"]
        else:
            arrays |= common | {"sums_before": sums}
            sums = call(functools.partial(beside_kernel, frames), "beside_rows", arrays, {"sums": sums_shape}, 3)["sums"]
        diagonal, sums = lax.optimization_barrier((diagonal, sums))
        arrays = with_other("diagonal", diagonal)
        if period == 0:
            away = {"tails_" + key: value for key, value in arrays.items()}
            seconds, sums = lax.optimization_barrier((seconds, sums))
            seconds[2] = lax.ppermute(seconds[2], "rows", across(count))
            seconds = with_other("seconds", jnp.concatenate(seconds, axis=0))
            arrays |= away
        arrays |= common | {"sums": sums}
        outs = {"out": tiles(3 * frames, channels)}
        middle = call(functools.partial(far_kernel, frames, base), "far_row", arrays, outs, 1)["out"]
        arrays = common | with_other("middle", middle) | {"source": source, "kept": kept}
        outs = {"out": tiles(frames, channels), "tails": tiles(2 * TAILS, channels)}
        if period:
            arrays |= {"older": out, "older_tails": tails, "cached_seconds": cached_seconds}
            if period < segments - 1:
                outs["result"] = tiles(frames, channels)
        else:
            arrays |= seconds
        second = call(functools.partial(second_kernel, frames, base, period, count), "second", arrays, outs, 3)
        out, tails = second["out"], second["tails"]
        if period < segments - 1:
            result = second["result"] if period else out
            source = lax.ppermute(result, "segment", [(i, (i + 1) % segments) for i in range(segments)])
            if period == 0:
                arrays, result = lax.optimization_barrier((common | cached | away | seconds, result))
                outs = {"cached_sums": tiles(6, channels, F32), "cached_seconds": tiles(2, channels, F32)}
                sums = call(cached_kernel, "cached_rows", arrays, outs, 8)
                cached_sums, cached_seconds = sums["cached_sums"], sums["cached_seconds"]
                source, cached_sums, cached_seconds = lax.optimization_barrier((source, cached_sums, cached_seconds))
    return (out[None, :, None], tails.reshape(1, 2, 2, 1, channels, LANES))


def solution(mesh):
    in_specs = (
        P(None, "rows", "chan", None),
        P("segment", None, None, "rows", "chan", None),
        P("segment", None, "chan", None, None, None, None),
        P("segment", None, None),
        P("segment", None, None),
    )
    out_specs = (
        P("segment", None, "rows", "chan", None),
        P("segment", None, None, "rows", "chan", None),
    )
    return jax.shard_map(shards, mesh=mesh, in_specs=in_specs, out_specs=out_specs, check_vma=False)
```

```python
import functools

import jax
import jax.numpy as jnp
from jax import lax
from jax.experimental import pallas as pl
from jax.experimental.pallas import tpu as pltpu
from jax.sharding import PartitionSpec as P

BF16 = jnp.bfloat16
F32 = jnp.float32
LANES = 128
MIB = 1024 * 1024
VMEM = pl.BlockSpec(memory_space=pltpu.VMEM)
SMEM = pl.BlockSpec(memory_space=pltpu.SMEM)
TAILS = 2


def params(mib):
    return pltpu.CompilerParams(vmem_limit_bytes=mib * MIB)


def turned(x, by):
    by = by % LANES
    return x if by == 0 else pltpu.roll(x, by, x.ndim - 1)


def tiles(count, channels, dtype=BF16):
    return jax.ShapeDtypeStruct((count, channels, LANES), dtype)


def prepared_kernel(place_ref, gain_ref, bias_ref, kernels_ref, gains_ref, biases_ref, all_ref):
    channels = biases_ref.shape[1]
    depth = gains_ref.shape[1]
    mine = pl.ds(pl.multiple_of(place_ref[0] * channels, channels), channels)
    for conv in range(2):
        for source, out in ((gain_ref, gains_ref.at[conv]), (bias_ref, all_ref)):
            for k in range(depth // LANES):
                at = slice(k * LANES, (k + 1) * LANES)
                out[at, :] = jnp.transpose(jnp.broadcast_to(source[conv : conv + 1, at], (LANES, LANES)))
        biases_ref[conv] = all_ref[mine, :]


def prepared(place, gain, bias, kernels, channels):
    depth = gain.shape[1]
    return pl.pallas_call(
        prepared_kernel,
        out_shape=(
            jax.ShapeDtypeStruct((2, depth, LANES), F32),
            jax.ShapeDtypeStruct((2, channels, LANES), F32),
        ),
        in_specs=[SMEM, VMEM, VMEM, VMEM],
        out_specs=(VMEM, VMEM),
        scratch_shapes=[pltpu.VMEM((depth, LANES), F32)],
        compiler_params=params(16),
        name="prepared",
    )(place, gain, bias, kernels)


class Part:
    def __init__(self, conv, ref):
        self.conv, self.ref = conv, ref
        self.window = ref["window"]
        self.weight = ref["weight"]
        _, self.taps, height, self.depth = self.weight.shape
        self.channels = height // 3
        self.mine_first = ref["place"][0] == 0
        self.side = ref["place"][1]
        self.lane = lax.broadcasted_iota(jnp.int32, (1, LANES), 1)

    def ordered(self, name, tile):
        own, other = self.ref[name][tile], self.ref[name + "_other"][tile]
        return [jnp.where(self.mine_first, own, other), jnp.where(self.mine_first, other, own)]

    def activate(self, slot, frame, name, tile, valid=None):
        values = [x.astype(F32) for x in self.ordered(name, tile)]
        square = sum(jnp.sum(v * v, axis=0, keepdims=True) for v in values)
        scale = 0.5 * lax.rsqrt(square / self.depth + 1e-06)
        if valid is not None:
            scale = jnp.where(valid, scale, 0.0)
        kept = []
        for h, value in enumerate(values):
            at = slice(h * self.channels, (h + 1) * self.channels)
            t = self.ref["gains"][self.conv, at, :] * value * scale
            active = (t + t * jnp.tanh(t)).astype(BF16)
            self.window[slot, frame + 2, at, :] = active
            kept.append(active)
        return jnp.where(self.mine_first, *kept)

    def cached(self, slot, name, tile):
        for f in range(2):
            for h, value in enumerate(self.ordered(name, tile + f)):
                self.window[slot, f, h * self.channels : (h + 1) * self.channels, :] = value

    def product(self, slots, first, frames, held=(True, True)):
        block, weight = [], []
        nothing = jnp.zeros((self.depth, LANES), BF16)
        for slot, tap in slots:
            row_tap = 1 + self.side * (tap - 1)
            for a in range(3):
                wanted = [first + f + a for f in range(frames)]
                here = [held[0 if frame < 2 else 1] for frame in wanted]
                if any(here):
                    tile = [self.window[slot, frame] if h else nothing for frame, h in zip(wanted, here)]
                    weight.append(self.weight[self.conv, 3 * a + row_tap])
                    block.append(jnp.concatenate(tile, axis=1))
        total = jnp.dot(
            jnp.concatenate(weight, axis=1), jnp.concatenate(block, axis=0), preferred_element_type=F32
        )
        sums = []
        for f in range(frames):
            left, centre, right = [
                total[d * self.channels : (d + 1) * self.channels, f * LANES : (f + 1) * LANES] for d in range(3)
            ]
            left = jnp.where(self.lane == 0, 0.0, turned(left, 1))
            right = jnp.where(self.lane == LANES - 1, 0.0, turned(right, -1))
            sums.append(left + centre + right)
        return sums


def near_kernel(frames, base, names, *refs):
    ref = dict(zip(names, refs))
    part = Part(0, ref)
    half = frames // 2
    bias = ref["biases"][0]
    places = [("own", 0), ("beside", 0), ("beside", 1), ("beside", 2)]

    def load(slot, first):
        name, group = places[slot]
        if first == 0:
            part.cached(slot, "tails_" + name, group * ref["tails_own"].shape[0])
        for f in range(first, first + half):
            kept = part.activate(slot, f, name, group * (frames + base) + base + f)
            if slot == 0 and f >= frames - 2:
                ref["kept"][f - frames + 2] = kept

    def store(q, slots, first):
        for f, value in enumerate(part.product(slots, first, half), first):
            ref["sums"][(q + 1) * frames + f] = value + bias

    for first in (0, half):
        load(0, first)
        load(1, first)
        store(0, [(1, 0), (0, 1)], first)
        load(2, first)
        store(-1, [(2, 0), (1, 1), (0, 2)], first)
        load(3, first)
        store(1, [(0, 0), (3, 2)], first)


def cached_kernel(names, *refs):
    ref = dict(zip(names, refs))
    first, second = Part(0, ref), Part(1, ref)
    tails = ref["tails_own"].shape[0]
    held = (True, False)
    first.cached(0, "tails_own", 0)
    for group in range(3):
        first.cached(1 + group, "tails_beside", group * tails)
    first.cached(4, "tails_diagonal", 0)
    for q, slots in ((-1, [(2, 0), (1, 1), (0, 2)]), (0, [(1, 0), (0, 1), (4, 2)]), (1, [(0, 0), (4, 1), (3, 2)])):
        for f, value in enumerate(first.product(slots, 0, 2, held)):
            ref["cached_sums"][2 * (q + 1) + f] = value + ref["biases"][0]
    for slot in range(3):
        second.cached(5 + slot, "seconds", TAILS * slot)
    for f, value in enumerate(second.product([(6, 0), (5, 1), (7, 2)], 0, 2, held)):
        ref["cached_seconds"][f] = value + ref["biases"][1]


def own_kernel(frames, names, *refs):
    ref = dict(zip(names, refs))
    part = Part(0, ref)
    half = frames // 2
    for first in (0, half):
        for f in range(first, first + half):
            kept = part.activate(0, f, "own", f)
            if f >= frames - 2:
                ref["kept"][f - frames + 2] = kept
        for q in (-1, 0, 1):
            for f, value in enumerate(part.product([(0, 1 - q)], first, half, (False, True)), first):
                before = ref["cached_sums"][2 * (q + 1) + f] if f < 2 else ref["biases"][0]
                ref["sums"][(q + 1) * frames + f] = value + before


def beside_kernel(frames, names, *refs):
    ref = dict(zip(names, refs))
    part = Part(0, ref)
    half = frames // 2

    def load(slot, first):
        for f in range(first, first + half):
            part.activate(slot, f, "beside", slot * frames + f)

    def store(q, slots, first):
        for f, value in enumerate(part.product(slots, first, half, (False, True)), first):
            at = (q + 1) * frames + f
            ref["sums"][at] = ref["sums_before"][at] + value

    for first in (0, half):
        load(0, first)
        store(0, [(0, 0)], first)
        load(1, first)
        store(-1, [(1, 0), (0, 1)], first)
        load(2, first)
        store(1, [(2, 2)], first)


def far_kernel(frames, base, names, *refs):
    ref = dict(zip(names, refs))
    part = Part(0, ref)
    half = frames // 2
    out, sums = ref["out"], ref["sums"]
    if base:
        part.cached(0, "tails_diagonal", 0)
    for first in (0, half):
        for f in range(first, first + half):
            part.activate(0, f, "diagonal", base + f)
            out[f] = sums[f].astype(BF16)
        for q, tap in ((0, 2), (1, 1)):
            for f, value in enumerate(part.product([(0, tap)], first, half, (base > 0, True)), first):
                at = (q + 1) * frames + f
                out[at] = (sums[at] + value).astype(BF16)


def second_kernel(frames, base, period, count, names, *refs):
    ref = dict(zip(names, refs))
    part = Part(1, ref)
    row, segment = ref["place"][2], ref["place"][3]
    bias = ref["biases"][1]
    offsets = (0, -1, 1)

    def load(first, last):
        for slot, q in enumerate(offsets):
            at = row + part.side * q
            valid = None if q == 0 else jnp.broadcast_to(jnp.logical_and(at >= 0, at < count), (1, LANES))
            for f in range(first, last):
                kept = part.activate(slot, f, "middle", (q + 1) * frames + f, valid)
                if slot == 0 and f >= frames - 2:
                    new_tails[2 + f - frames + 2] = kept

    new_tails = {f: ref["kept"][f] for f in range(2)}

    def store(first, last):
        sums = part.product([(1, 0), (0, 1), (2, 2)], first, last - first, (period == 0, True))
        for f, value in enumerate(sums, first):
            before = ref["cached_seconds"][f] if period and f < 2 else bias
            result = (ref["source"][base + f].astype(F32) + (value + before)).astype(BF16)
            if "result" in ref:
                ref["result"][f] = result
            ref["out"][f] = jnp.where(segment == period, result, ref["older"][f]) if period else result

    if period == 0:
        for slot in range(len(offsets)):
            part.cached(slot, "seconds", TAILS * slot)
    half = frames // 2
    load(0, half)
    store(0, half)
    load(half, frames)
    store(half, frames)
    for f in range(4):
        tail = new_tails[f]
        ref["tails"][f] = jnp.where(segment == period, tail, ref["older_tails"][f]) if period else tail


def call(kernel, name, arrays, outs, slots):
    depth = arrays["weight"].shape[-1]
    frames = 4
    scratch = {"window": pltpu.VMEM((slots, frames + 2, depth, LANES), BF16)}
    names = [*arrays, *outs, *scratch]
    results = pl.pallas_call(
        functools.partial(kernel, names),
        out_shape=list(outs.values()),
        in_specs=[SMEM if key == "place" else VMEM for key in arrays],
        out_specs=[VMEM] * len(outs),
        scratch_shapes=list(scratch.values()),
        compiler_params=params(16),
        name=name,
    )(*arrays.values())
    return dict(zip(outs, results))


def swapped(x):
    return lax.ppermute(x, "chan", [(0, 1), (1, 0)])


def with_other(name, x):
    return {name: x, name + "_other": swapped(x)}


def across(count):
    return [(i, i ^ 1) for i in range(count)]


def exchanged(x, x_later, count):
    pairs = count // 2
    even, odd = [], []
    for i in range(count):
        k = i // 2
        for k_to, group in ((k ^ 1, even), (k + 1 if k % 2 else k - 1, odd)):
            if 0 <= k_to < pairs:
                group.append((i, 2 * k_to + i % 2))
    even, odd = [lax.ppermute(x, "rows", pairs) for pairs in (even, odd)]
    return lax.ppermute(x_later, "rows", across(count)), even, odd


def shards(features, caches, conv_weights, conv_bias, norm_gain):
    count = lax.axis_size("rows")
    segments = lax.axis_size("segment")
    row = lax.axis_index("rows")
    frames, _, channels, _ = features.shape
    depth = conv_weights.shape[-1]
    kernels = jnp.transpose(conv_weights[0], (0, 2, 3, 4, 1, 5)).reshape(2, 9, 3 * channels, depth)
    kind, pair = row % 2, row // 2
    place = [lax.axis_index("chan"), 2 * kind - 1, row, lax.axis_index("segment")]
    place = jnp.stack(place).astype(jnp.int32)

    source = jnp.concatenate([caches[0].reshape(2 * TAILS, channels, LANES), features[:, 0]], axis=0)
    gains, biases = prepared(place, norm_gain[0], conv_bias[0], kernels, channels)
    source = jnp.concatenate([caches[0].reshape(2 * TAILS, channels, LANES), features[:, 0]], axis=0)
    sums_shape, kept_shape = tiles(3 * frames, channels, F32), tiles(2, channels)
    near_first = kind == pair % 2
    out = tails = cached_seconds = None
    for period in range(segments):
        base = 0 if period else TAILS
        own = with_other("own", source)
        source, own["own_other"] = lax.optimization_barrier((source, own["own_other"]))
        beside, even, odd = exchanged(own["own"], own["own"] if period else source, count)
        if period == 0:
            even, odd, gains, biases = lax.optimization_barrier((even, odd, gains, biases))
            common = {"place": place, "gains": gains, "biases": biases, "weight": kernels}
        else:
            arrays = common | own | {"cached_sums": cached_sums}
            outs = {"sums": sums_shape, "kept": kept_shape}
            first = call(functools.partial(own_kernel, frames), "own_row", arrays, outs, 1)
            sums, kept = first["sums"], first["kept"]
            even, odd, sums, kept = lax.optimization_barrier((even, odd, sums, kept))
        near, far = jnp.where(near_first, even, odd), jnp.where(near_first, odd, even)
        if period == 0:
            seconds = [x[TAILS : 2 * TAILS] for x in (source, beside, near)]
            source, beside, near, far = [
                jnp.concatenate([x[:TAILS], x[2 * TAILS :]], axis=0) for x in (source, beside, near, far)
            ]
        diagonal = lax.ppermute(near, "rows", across(count))
        arrays = with_other("beside", jnp.concatenate([beside, near, far], axis=0))
        if period == 0:
            arrays |= with_other("own", source)
            cached = {"tails_" + key: value for key, value in arrays.items()}
            outs = {"sums": sums_shape, "kept": kept_shape}
            first = call(functools.partial(near_kernel, frames, base), "near_rows", common | arrays | cached, outs, 4)
            sums, kept = first["sums"], first["kept"]
        else:
            arrays |= common | {"sums_before": sums}
            sums = call(functools.partial(beside_kernel, frames), "beside_rows", arrays, {"sums": sums_shape}, 3)["sums"]
        diagonal, sums = lax.optimization_barrier((diagonal, sums))
        arrays = with_other("diagonal", diagonal)
        if period == 0:
            away = {"tails_" + key: value for key, value in arrays.items()}
            seconds, sums = lax.optimization_barrier((seconds, sums))
            seconds[2] = lax.ppermute(seconds[2], "rows", across(count))
            seconds = with_other("seconds", jnp.concatenate(seconds, axis=0))
            arrays |= away
        arrays |= common | {"sums": sums}
        outs = {"out": tiles(3 * frames, channels)}
        middle = call(functools.partial(far_kernel, frames, base), "far_row", arrays, outs, 1)["out"]
        arrays = common | with_other("middle", middle) | {"source": source, "kept": kept}
        outs = {"out": tiles(frames, channels), "tails": tiles(2 * TAILS, channels)}
        if period:
            arrays |= {"older": out, "older_tails": tails, "cached_seconds": cached_seconds}
            if period < segments - 1:
                outs["result"] = tiles(frames, channels)
        else:
            arrays |= seconds
        second = call(functools.partial(second_kernel, frames, base, period, count), "second", arrays, outs, 3)
        out, tails = second["out"], second["tails"]
        if period < segments - 1:
            result = second["result"] if period else out
            source = lax.ppermute(result, "segment", [(i, (i + 1) % segments) for i in range(segments)])
            if period == 0:
                arrays, result = lax.optimization_barrier((common | cached | away | seconds, result))
                outs = {"cached_sums": tiles(6, channels, F32), "cached_seconds": tiles(2, channels, F32)}
                sums = call(cached_kernel, "cached_rows", arrays, outs, 8)
                cached_sums, cached_seconds = sums["cached_sums"], sums["cached_seconds"]
                source, cached_sums, cached_seconds = lax.optimization_barrier((source, cached_sums, cached_seconds))
    return (out[None, :, None], tails.reshape(1, 2, 2, 1, channels, LANES))


def solution(mesh):
    in_specs = (
        P(None, "rows", "chan", None),
        P("segment", None, None, "rows", "chan", None),
        P("segment", None, "chan", None, None, None, None),
        P("segment", None, None),
        P("segment", None, None),
    )
    out_specs = (
        P("segment", None, "rows", "chan", None),
        P("segment", None, None, "rows", "chan", None),
    )
    return jax.shard_map(shards, mesh=mesh, in_specs=in_specs, out_specs=out_specs, check_vma=False)
```

```python
import functools

import jax
import jax.numpy as jnp
from jax import lax
from jax.experimental import pallas as pl
from jax.experimental.pallas import tpu as pltpu
from jax.sharding import PartitionSpec as P

BF16 = jnp.bfloat16
F32 = jnp.float32
LANES = 128
MIB = 1024 * 1024
VMEM = pl.BlockSpec(memory_space=pltpu.VMEM)
SMEM = pl.BlockSpec(memory_space=pltpu.SMEM)
TAILS = 2
FRAMES = 4


def params(mib):
    return pltpu.CompilerParams(vmem_limit_bytes=mib * MIB)


def turned(x, by):
    by = by % LANES
    return x if by == 0 else pltpu.roll(x, by, x.ndim - 1)


def tiles(count, channels, dtype=BF16):
    return jax.ShapeDtypeStruct((count, channels, LANES), dtype)


def prepared_kernel(place_ref, gain_ref, bias_ref, kernels_ref, gains_ref, biases_ref, all_ref):
    channels = biases_ref.shape[1]
    depth = gains_ref.shape[1]
    mine = pl.ds(pl.multiple_of(place_ref[0] * channels, channels), channels)
    for conv in range(2):
        for source, out in ((gain_ref, gains_ref.at[conv]), (bias_ref, all_ref)):
            for k in range(depth // LANES):
                at = slice(k * LANES, (k + 1) * LANES)
                out[at, :] = jnp.transpose(jnp.broadcast_to(source[conv : conv + 1, at], (LANES, LANES)))
        biases_ref[conv] = all_ref[mine, :]


def prepared(place, gain, bias, kernels, channels):
    depth = gain.shape[1]
    return pl.pallas_call(
        prepared_kernel,
        out_shape=(
            jax.ShapeDtypeStruct((2, depth, LANES), F32),
            jax.ShapeDtypeStruct((2, channels, LANES), F32),
        ),
        in_specs=[SMEM, VMEM, VMEM, VMEM],
        out_specs=(VMEM, VMEM),
        scratch_shapes=[pltpu.VMEM((depth, LANES), F32)],
        compiler_params=params(16),
        name="prepared",
    )(place, gain, bias, kernels)


class Part:
    def __init__(self, conv, ref):
        self.conv, self.ref = conv, ref
        self.window = ref["window"]
        self.weight = ref["weight"]
        _, self.taps, height, self.depth = self.weight.shape
        self.channels = height // 3
        self.mine_first = ref["place"][0] == 0
        self.side = ref["place"][1]
        self.lane = lax.broadcasted_iota(jnp.int32, (1, LANES), 1)

    def ordered(self, name, tile):
        own, other = self.ref[name][tile], self.ref[name + "_other"][tile]
        return [jnp.where(self.mine_first, own, other), jnp.where(self.mine_first, other, own)]

    def activate(self, slot, frame, name, tile, valid=None):
        values = [x.astype(F32) for x in self.ordered(name, tile)]
        square = sum(jnp.sum(v * v, axis=0, keepdims=True) for v in values)
        scale = 0.5 * lax.rsqrt(square / self.depth + 1e-06)
        if valid is not None:
            scale = jnp.where(valid, scale, 0.0)
        kept = []
        for h, value in enumerate(values):
            at = slice(h * self.channels, (h + 1) * self.channels)
            t = self.ref["gains"][self.conv, at, :] * value * scale
            active = (t + t * jnp.tanh(t)).astype(BF16)
            self.window[slot, frame + 2, at, :] = active
            kept.append(active)
        return jnp.where(self.mine_first, *kept)

    def cached(self, slot, name, tile):
        for f in range(2):
            for h, value in enumerate(self.ordered(name, tile + f)):
                self.window[slot, f, h * self.channels : (h + 1) * self.channels, :] = value

    def product(self, slots, first, frames, held=(True, True)):
        block, weight = [], []
        nothing = jnp.zeros((self.depth, LANES), BF16)
        for slot, tap in slots:
            row_tap = 1 + self.side * (tap - 1)
            for a in range(3):
                wanted = [first + f + a for f in range(frames)]
                here = [held[0 if frame < 2 else 1] for frame in wanted]
                if any(here):
                    tile = [self.window[slot, frame] if h else nothing for frame, h in zip(wanted, here)]
                    weight.append(self.weight[self.conv, 3 * a + row_tap])
                    block.append(jnp.concatenate(tile, axis=1))
        total = jnp.dot(
            jnp.concatenate(weight, axis=1), jnp.concatenate(block, axis=0), preferred_element_type=F32
        )
        sums = []
        for f in range(frames):
            left, centre, right = [
                total[d * self.channels : (d + 1) * self.channels, f * LANES : (f + 1) * LANES] for d in range(3)
            ]
            left = jnp.where(self.lane == 0, 0.0, turned(left, 1))
            right = jnp.where(self.lane == LANES - 1, 0.0, turned(right, -1))
            sums.append(left + centre + right)
        return sums


def cached_kernel(names, *refs):
    ref = dict(zip(names, refs))
    first, second = Part(0, ref), Part(1, ref)
    held = (True, False)
    row = TAILS + FRAMES
    places = (("own", 0), ("beside", 0), ("pairs", 0), ("pairs", row), ("diagonal", 0))
    for slot, (name, tile) in enumerate(places):
        first.cached(slot, name, tile)
    for q, slots in ((-1, [(2, 0), (1, 1), (0, 2)]), (0, [(1, 0), (0, 1), (4, 2)]), (1, [(0, 0), (4, 1), (3, 2)])):
        for f, value in enumerate(first.product(slots, 0, 2, held)):
            ref["cached_sums"][2 * (q + 1) + f] = value + ref["biases"][0]
    for slot in range(3):
        second.cached(5 + slot, "seconds", TAILS * slot)
    for f, value in enumerate(second.product([(6, 0), (5, 1), (7, 2)], 0, 2, held)):
        ref["cached_seconds"][f] = value + ref["biases"][1]


def own_kernel(frames, base, names, *refs):
    ref = dict(zip(names, refs))
    part = Part(0, ref)
    half = frames // 2
    if base:
        part.cached(0, "own", 0)
    for first in (0, half):
        for f in range(first, first + half):
            kept = part.activate(0, f, "own", base + f)
            if f >= frames - 2:
                ref["kept"][f - frames + 2] = kept
        for q in (-1, 0, 1):
            for f, value in enumerate(part.product([(0, 1 - q)], first, half, (base > 0, True)), first):
                before = ref["biases"][0] if base or f >= 2 else ref["cached_sums"][2 * (q + 1) + f]
                ref["sums"][(q + 1) * frames + f] = value + before


def beside_kernel(frames, base, names, *refs):
    ref = dict(zip(names, refs))
    part = Part(0, ref)
    half = frames // 2
    places = (("beside", 0), ("pairs", 0), ("pairs", base + frames))

    def load(slot, first):
        name, tile = places[slot]
        if base and first == 0:
            part.cached(slot, name, tile)
        for f in range(first, first + half):
            part.activate(slot, f, name, tile + base + f)

    def store(q, slots, first):
        for f, value in enumerate(part.product(slots, first, half, (base > 0, True)), first):
            at = (q + 1) * frames + f
            ref["sums"][at] = ref["sums_before"][at] + value

    for first in (0, half):
        load(0, first)
        store(0, [(0, 0)], first)
        load(1, first)
        store(-1, [(1, 0), (0, 1)], first)
        load(2, first)
        store(1, [(2, 2)], first)


def far_kernel(frames, base, names, *refs):
    ref = dict(zip(names, refs))
    part = Part(0, ref)
    half = frames // 2
    out, sums = ref["out"], ref["sums"]
    if base:
        part.cached(0, "diagonal", 0)
    for first in (0, half):
        for f in range(first, first + half):
            part.activate(0, f, "diagonal", base + f)
            out[f] = sums[f].astype(BF16)
        for q, tap in ((0, 2), (1, 1)):
            for f, value in enumerate(part.product([(0, tap)], first, half, (base > 0, True)), first):
                at = (q + 1) * frames + f
                out[at] = (sums[at] + value).astype(BF16)


def second_kernel(frames, base, period, count, names, *refs):
    ref = dict(zip(names, refs))
    part = Part(1, ref)
    row, segment = ref["place"][2], ref["place"][3]
    bias = ref["biases"][1]
    offsets = (0, -1, 1)

    def load(first, last):
        for slot, q in enumerate(offsets):
            at = row + part.side * q
            valid = None if q == 0 else jnp.broadcast_to(jnp.logical_and(at >= 0, at < count), (1, LANES))
            for f in range(first, last):
                kept = part.activate(slot, f, "middle", (q + 1) * frames + f, valid)
                if slot == 0 and f >= frames - 2:
                    new_tails[2 + f - frames + 2] = kept

    new_tails = {f: ref["kept"][f] for f in range(2)}

    def store(first, last):
        sums = part.product([(1, 0), (0, 1), (2, 2)], first, last - first, (period == 0, True))
        for f, value in enumerate(sums, first):
            before = ref["cached_seconds"][f] if period and f < 2 else bias
            result = (ref["own"][base + f].astype(F32) + (value + before)).astype(BF16)
            if "result" in ref:
                ref["result"][f] = result
            ref["out"][f] = jnp.where(segment == period, result, ref["older"][f]) if period else result

    if period == 0:
        for slot in range(len(offsets)):
            part.cached(slot, "seconds", TAILS * slot)
    half = frames // 2
    load(0, half)
    store(0, half)
    load(half, frames)
    store(half, frames)
    for f in range(4):
        tail = new_tails[f]
        ref["tails"][f] = jnp.where(segment == period, tail, ref["older_tails"][f]) if period else tail


def call(kernel, name, arrays, outs, slots):
    depth = arrays["weight"].shape[-1]
    scratch = {"window": pltpu.VMEM((slots, FRAMES + 2, depth, LANES), BF16)}
    names = [*arrays, *outs, *scratch]
    results = pl.pallas_call(
        functools.partial(kernel, names),
        out_shape=list(outs.values()),
        in_specs=[SMEM if key == "place" else VMEM for key in arrays],
        out_specs=[VMEM] * len(outs),
        scratch_shapes=list(scratch.values()),
        compiler_params=params(16),
        name=name,
    )(*arrays.values())
    return dict(zip(outs, results))


def swapped(x):
    return lax.ppermute(x, "chan", [(0, 1), (1, 0)])


def with_other(name, x):
    return {name: x, name + "_other": swapped(x)}


def across(count):
    return [(i, i ^ 1) for i in range(count)]


def exchanged(x, count):
    pairs = count // 2
    even, odd = [], []
    for i in range(count):
        k = i // 2
        for k_to, group in ((k ^ 1, odd), (k + 1 if k % 2 else k - 1, even)):
            if 0 <= k_to < pairs:
                group.append((i, 2 * k_to + i % 2))
    return [lax.ppermute(x, "rows", pairs) for pairs in (across(count), even, odd)]


def shards(features, caches, conv_weights, conv_bias, norm_gain):
    count = lax.axis_size("rows")
    segments = lax.axis_size("segment")
    row = lax.axis_index("rows")
    frames, _, channels, _ = features.shape
    depth = conv_weights.shape[-1]
    kernels = jnp.transpose(conv_weights[0], (0, 2, 3, 4, 1, 5)).reshape(2, 9, 3 * channels, depth)
    kind, pair = row % 2, row // 2
    place = [lax.axis_index("chan"), 2 * kind - 1, row, lax.axis_index("segment")]
    place = jnp.stack(place).astype(jnp.int32)

    source = jnp.concatenate([caches[0].reshape(2 * TAILS, channels, LANES), features[:, 0]], axis=0)
    gains, biases = prepared(place, norm_gain[0], conv_bias[0], kernels, channels)
    source = jnp.concatenate([caches[0].reshape(2 * TAILS, channels, LANES), features[:, 0]], axis=0)
    sums_shape, kept_shape = tiles(3 * frames, channels, F32), tiles(2, channels)
    near_first = kind != pair % 2
    out = tails = cached_seconds = None
    for period in range(segments):
        base = 0 if period else TAILS
        beside, even, odd = exchanged(source, count)
        if period == 0:
            even, odd, gains, biases = lax.optimization_barrier((even, odd, gains, biases))
            common = {"place": place, "gains": gains, "biases": biases, "weight": kernels}
        near, far = jnp.where(near_first, even, odd), jnp.where(near_first, odd, even)
        if period == 0:
            seconds = [x[TAILS : 2 * TAILS] for x in (source, beside, near)]
            source, beside, near, far = [
                jnp.concatenate([x[:TAILS], x[2 * TAILS :]], axis=0) for x in (source, beside, near, far)
            ]
        own = with_other("own", source)
        diagonal = lax.ppermute(near, "rows", across(count))
        pairs = jnp.concatenate([near, far], axis=0)
        own["own_other"], beside, pairs = lax.optimization_barrier((own["own_other"], beside, pairs))
        beside = with_other("beside", beside) | with_other("pairs", pairs)
        arrays = common | own | ({"cached_sums": cached_sums} if period else {})
        outs = {"sums": sums_shape, "kept": kept_shape}
        first = call(functools.partial(own_kernel, frames, base), "own_row", arrays, outs, 1)
        arrays = common | beside | {"sums_before": first["sums"]}
        kernel = functools.partial(beside_kernel, frames, base)
        sums = call(kernel, "beside_rows", arrays, {"sums": sums_shape}, 3)["sums"]
        diagonal, sums = lax.optimization_barrier((diagonal, sums))
        diagonal = with_other("diagonal", diagonal)
        if period == 0:
            seconds, sums = lax.optimization_barrier((seconds, sums))
            seconds[2] = lax.ppermute(seconds[2], "rows", across(count))
            seconds = with_other("seconds", jnp.concatenate(seconds, axis=0))
        arrays = common | diagonal | {"sums": sums}
        outs = {"out": tiles(3 * frames, channels)}
        middle = call(functools.partial(far_kernel, frames, base), "far_row", arrays, outs, 1)["out"]
        arrays = common | with_other("middle", middle) | {"own": own["own"], "kept": first["kept"]}
        outs = {"out": tiles(frames, channels), "tails": tiles(2 * TAILS, channels)}
        if period:
            arrays |= {"older": out, "older_tails": tails, "cached_seconds": cached_seconds}
            if period < segments - 1:
                outs["result"] = tiles(frames, channels)
        else:
            arrays |= seconds
        second = call(functools.partial(second_kernel, frames, base, period, count), "second", arrays, outs, 3)
        out, tails = second["out"], second["tails"]
        if period < segments - 1:
            result = second["result"] if period else out
            source = lax.ppermute(result, "segment", [(i, (i + 1) % segments) for i in range(segments)])
            if period == 0:
                arrays, result = lax.optimization_barrier((common | own | beside | diagonal | seconds, result))
                outs = {"cached_sums": tiles(6, channels, F32), "cached_seconds": tiles(2, channels, F32)}
                sums = call(cached_kernel, "cached_rows", arrays, outs, 8)
                cached_sums, cached_seconds = sums["cached_sums"], sums["cached_seconds"]
                source, cached_sums, cached_seconds = lax.optimization_barrier((source, cached_sums, cached_seconds))
    return (out[None, :, None], tails.reshape(1, 2, 2, 1, channels, LANES))


def solution(mesh):
    in_specs = (
        P(None, "rows", "chan", None),
        P("segment", None, None, "rows", "chan", None),
        P("segment", None, "chan", None, None, None, None),
        P("segment", None, None),
        P("segment", None, None),
    )
    out_specs = (
        P("segment", None, "rows", "chan", None),
        P("segment", None, None, "rows", "chan", None),
    )
    return jax.shard_map(shards, mesh=mesh, in_specs=in_specs, out_specs=out_specs, check_vma=False)
```

```python
import functools

import jax
import jax.numpy as jnp
from jax import lax
from jax.experimental import pallas as pl
from jax.experimental.pallas import tpu as pltpu
from jax.sharding import PartitionSpec as P

BF16 = jnp.bfloat16
F32 = jnp.float32
LANES = 128
MIB = 1024 * 1024
VMEM = pl.BlockSpec(memory_space=pltpu.VMEM)
SMEM = pl.BlockSpec(memory_space=pltpu.SMEM)
TAILS = 2
FRAMES = 4


def params(mib):
    return pltpu.CompilerParams(vmem_limit_bytes=mib * MIB)


def turned(x, by):
    by = by % LANES
    return x if by == 0 else pltpu.roll(x, by, x.ndim - 1)


def tiles(count, channels, dtype=BF16):
    return jax.ShapeDtypeStruct((count, channels, LANES), dtype)


def prepared_kernel(place_ref, gain_ref, bias_ref, kernels_ref, gains_ref, biases_ref, all_ref):
    channels = biases_ref.shape[1]
    depth = gains_ref.shape[1]
    mine = pl.ds(pl.multiple_of(place_ref[0] * channels, channels), channels)
    for conv in range(2):
        for source, out in ((gain_ref, gains_ref.at[conv]), (bias_ref, all_ref)):
            for k in range(depth // LANES):
                at = slice(k * LANES, (k + 1) * LANES)
                out[at, :] = jnp.transpose(jnp.broadcast_to(source[conv : conv + 1, at], (LANES, LANES)))
        biases_ref[conv] = all_ref[mine, :]


def prepared(place, gain, bias, kernels, channels):
    depth = gain.shape[1]
    return pl.pallas_call(
        prepared_kernel,
        out_shape=(
            jax.ShapeDtypeStruct((2, depth, LANES), F32),
            jax.ShapeDtypeStruct((2, channels, LANES), F32),
        ),
        in_specs=[SMEM, VMEM, VMEM, VMEM],
        out_specs=(VMEM, VMEM),
        scratch_shapes=[pltpu.VMEM((depth, LANES), F32)],
        compiler_params=params(16),
        name="prepared",
    )(place, gain, bias, kernels)


class Part:
    def __init__(self, conv, ref):
        self.conv, self.ref = conv, ref
        self.window = ref["window"]
        self.weight = ref["weight"]
        _, self.taps, height, self.depth = self.weight.shape
        self.channels = height // 3
        self.mine_first = ref["place"][0] == 0
        self.side = ref["place"][1]
        self.lane = lax.broadcasted_iota(jnp.int32, (1, LANES), 1)

    def ordered(self, name, tile):
        own, other = self.ref[name][tile], self.ref[name + "_other"][tile]
        return [jnp.where(self.mine_first, own, other), jnp.where(self.mine_first, other, own)]

    def activate(self, slot, frame, name, tile, valid=None):
        values = [x.astype(F32) for x in self.ordered(name, tile)]
        square = sum(jnp.sum(v * v, axis=0, keepdims=True) for v in values)
        scale = 0.5 * lax.rsqrt(square / self.depth + 1e-06)
        if valid is not None:
            scale = jnp.where(valid, scale, 0.0)
        kept = []
        for h, value in enumerate(values):
            at = slice(h * self.channels, (h + 1) * self.channels)
            t = self.ref["gains"][self.conv, at, :] * value * scale
            active = (t + t * jnp.tanh(t)).astype(BF16)
            self.window[slot, frame + 2, at, :] = active
            kept.append(active)
        return jnp.where(self.mine_first, *kept)

    def cached(self, slot, name, tile):
        for f in range(2):
            for h, value in enumerate(self.ordered(name, tile + f)):
                self.window[slot, f, h * self.channels : (h + 1) * self.channels, :] = value

    def product(self, slots, first, frames, held=(True, True)):
        block, weight = [], []
        nothing = jnp.zeros((self.depth, LANES), BF16)
        for slot, tap, *held_here in slots:
            held_now = held_here[0] if held_here else held
            row_tap = 1 + self.side * (tap - 1)
            for a in range(3):
                wanted = [first + f + a for f in range(frames)]
                here = [held_now[0 if frame < 2 else 1] for frame in wanted]
                if any(here):
                    tile = [self.window[slot, frame] if h else nothing for frame, h in zip(wanted, here)]
                    weight.append(self.weight[self.conv, 3 * a + row_tap])
                    block.append(jnp.concatenate(tile, axis=1))
        total = jnp.dot(
            jnp.concatenate(weight, axis=1), jnp.concatenate(block, axis=0), preferred_element_type=F32
        )
        sums = []
        for f in range(frames):
            left, centre, right = [
                total[d * self.channels : (d + 1) * self.channels, f * LANES : (f + 1) * LANES] for d in range(3)
            ]
            left = jnp.where(self.lane == 0, 0.0, turned(left, 1))
            right = jnp.where(self.lane == LANES - 1, 0.0, turned(right, -1))
            sums.append(left + centre + right)
        return sums


def cached_kernel(names, *refs):
    ref = dict(zip(names, refs))
    first, second = Part(0, ref), Part(1, ref)
    held = (True, False)
    row = TAILS + FRAMES
    places = (("own", 0), ("beside", 0), ("pairs", 0), ("pairs", row), ("diagonal", 0))
    for slot, (name, tile) in enumerate(places):
        first.cached(slot, name, tile)
    for q, slots in ((-1, [(2, 0), (1, 1), (0, 2)]), (0, [(1, 0), (0, 1), (4, 2)]), (1, [(0, 0), (4, 1), (3, 2)])):
        for f, value in enumerate(first.product(slots, 0, 2, held)):
            ref["cached_sums"][2 * (q + 1) + f] = value + ref["biases"][0]
    for slot in range(3):
        second.cached(5 + slot, "seconds", TAILS * slot)
    for f, value in enumerate(second.product([(6, 0), (5, 1), (7, 2)], 0, 2, held)):
        ref["cached_seconds"][f] = value + ref["biases"][1]


def own_kernel(frames, base, names, *refs):
    ref = dict(zip(names, refs))
    part = Part(0, ref)
    half = frames // 2
    if base:
        part.cached(0, "own", 0)
    for first in (0, half):
        for f in range(first, first + half):
            kept = part.activate(0, f, "own", base + f)
            if f >= frames - 2:
                ref["kept"][f - frames + 2] = kept
        for q in (-1, 0, 1):
            for f, value in enumerate(part.product([(0, 1 - q)], first, half, (base > 0, True)), first):
                before = ref["biases"][0] if base or f >= 2 else ref["cached_sums"][2 * (q + 1) + f]
                ref["sums"][(q + 1) * frames + f] = value + before


def beside_kernel(frames, base, names, *refs):
    ref = dict(zip(names, refs))
    part = Part(0, ref)
    half = frames // 2
    places = (("beside", 0), ("pairs", 0), ("pairs", base + frames))

    def load(slot, first):
        name, tile = places[slot]
        if base and first == 0:
            part.cached(slot, name, tile)
        for f in range(first, first + half):
            part.activate(slot, f, name, tile + base + f)

    def store(q, slots, first):
        for f, value in enumerate(part.product(slots, first, half, (base > 0, True)), first):
            total = ref["sums_before"][(q + 1) * frames + f] + value
            if q < 0:
                ref["first"][f] = total.astype(BF16)
            else:
                ref["sums"][q * frames + f] = total

    for first in (0, half):
        load(0, first)
        store(0, [(0, 0)], first)
        load(1, first)
        store(-1, [(1, 0), (0, 1)], first)
        load(2, first)
        store(1, [(2, 2)], first)


def far_kernel(frames, base, names, *refs):
    ref = dict(zip(names, refs))
    part = Part(0, ref)
    half = frames // 2
    out, sums = ref["out"], ref["sums"]
    if base:
        part.cached(0, "diagonal", 0)
    for first in (0, half):
        for f in range(first, first + half):
            part.activate(0, f, "diagonal", base + f)
        for q, tap in ((0, 2), (1, 1)):
            for f, value in enumerate(part.product([(0, tap)], first, half, (base > 0, True)), first):
                at = q * frames + f
                out[at] = (sums[at] + value).astype(BF16)


def inside(part, count, q):
    at = part.ref["place"][2] + part.side * q
    return jnp.broadcast_to(jnp.logical_and(at >= 0, at < count), (1, LANES))


def second_ahead_kernel(frames, count, names, *refs):
    ref = dict(zip(names, refs))
    part = Part(1, ref)
    half = frames // 2
    for first in (0, half):
        for f in range(first, first + half):
            part.activate(0, f, "first", f, inside(part, count, -1))
        for f, value in enumerate(part.product([(0, 0)], first, half, (False, True)), first):
            ref["ahead"][f] = value


def second_kernel(frames, base, period, count, names, *refs):
    ref = dict(zip(names, refs))
    part = Part(1, ref)
    segment = ref["place"][3]
    bias = ref["biases"][1]
    half = frames // 2
    slots = [(0, 1), (1, 2)]
    if period == 0:
        for slot, place in enumerate((0, 2, 1)):
            part.cached(slot, "seconds", TAILS * place)
        slots.append((2, 0, (True, False)))
    tails = {f: ref["kept"][f] for f in range(2)}
    for first in (0, half):
        for q in range(2):
            for f in range(first, first + half):
                kept = part.activate(q, f, "middle", q * frames + f, inside(part, count, q) if q else None)
                if q == 0 and f >= frames - 2:
                    tails[4 + f - frames] = kept
        for f, value in enumerate(part.product(slots, first, half, (period == 0, True)), first):
            before = ref["cached_seconds"][f] if period and f < 2 else bias
            total = value + ref["ahead"][f] + before
            result = (ref["own"][base + f].astype(F32) + total).astype(BF16)
            if "result" in ref:
                ref["result"][f] = result
            ref["out"][f] = jnp.where(segment == period, result, ref["older"][f]) if period else result
    for f, tail in tails.items():
        ref["tails"][f] = jnp.where(segment == period, tail, ref["older_tails"][f]) if period else tail


def call(kernel, name, arrays, outs, slots):
    depth = arrays["weight"].shape[-1]
    scratch = {"window": pltpu.VMEM((slots, FRAMES + 2, depth, LANES), BF16)}
    names = [*arrays, *outs, *scratch]
    results = pl.pallas_call(
        functools.partial(kernel, names),
        out_shape=list(outs.values()),
        in_specs=[SMEM if key == "place" else VMEM for key in arrays],
        out_specs=[VMEM] * len(outs),
        scratch_shapes=list(scratch.values()),
        compiler_params=params(16),
        name=name,
    )(*arrays.values())
    return dict(zip(outs, results))


def swapped(x):
    return lax.ppermute(x, "chan", [(0, 1), (1, 0)])


def with_other(name, x):
    return {name: x, name + "_other": swapped(x)}


def across(count):
    return [(i, i ^ 1) for i in range(count)]


def exchanged(x, count):
    pairs = count // 2
    even, odd = [], []
    for i in range(count):
        k = i // 2
        for k_to, group in ((k ^ 1, odd), (k + 1 if k % 2 else k - 1, even)):
            if 0 <= k_to < pairs:
                group.append((i, 2 * k_to + i % 2))
    return [lax.ppermute(x, "rows", pairs) for pairs in (across(count), even, odd)]


def shards(features, caches, conv_weights, conv_bias, norm_gain):
    count = lax.axis_size("rows")
    segments = lax.axis_size("segment")
    row = lax.axis_index("rows")
    frames, _, channels, _ = features.shape
    depth = conv_weights.shape[-1]
    kernels = jnp.transpose(conv_weights[0], (0, 2, 3, 4, 1, 5)).reshape(2, 9, 3 * channels, depth)
    kind, pair = row % 2, row // 2
    place = [lax.axis_index("chan"), 2 * kind - 1, row, lax.axis_index("segment")]
    place = jnp.stack(place).astype(jnp.int32)

    source = jnp.concatenate([caches[0].reshape(2 * TAILS, channels, LANES), features[:, 0]], axis=0)
    gains, biases = prepared(place, norm_gain[0], conv_bias[0], kernels, channels)
    source = jnp.concatenate([caches[0].reshape(2 * TAILS, channels, LANES), features[:, 0]], axis=0)
    sums_shape, kept_shape = tiles(3 * frames, channels, F32), tiles(2, channels)
    near_first = kind != pair % 2
    out = tails = cached_seconds = None
    for period in range(segments):
        base = 0 if period else TAILS
        beside, even, odd = exchanged(source, count)
        if period == 0:
            even, odd, gains, biases = lax.optimization_barrier((even, odd, gains, biases))
            common = {"place": place, "gains": gains, "biases": biases, "weight": kernels}
        near, far = jnp.where(near_first, even, odd), jnp.where(near_first, odd, even)
        if period == 0:
            seconds = [x[TAILS : 2 * TAILS] for x in (source, beside, near)]
            source, beside, near, far = [
                jnp.concatenate([x[:TAILS], x[2 * TAILS :]], axis=0) for x in (source, beside, near, far)
            ]
        own = with_other("own", source)
        diagonal = lax.ppermute(near, "rows", across(count))
        pairs = jnp.concatenate([near, far], axis=0)
        own["own_other"], beside, pairs = lax.optimization_barrier((own["own_other"], beside, pairs))
        beside = with_other("beside", beside) | with_other("pairs", pairs)
        arrays = common | own | ({"cached_sums": cached_sums} if period else {})
        outs = {"sums": sums_shape, "kept": kept_shape}
        first = call(functools.partial(own_kernel, frames, base), "own_row", arrays, outs, 1)
        arrays = common | beside | {"sums_before": first["sums"]}
        kernel = functools.partial(beside_kernel, frames, base)
        outs = {"sums": tiles(2 * frames, channels, F32), "first": tiles(frames, channels)}
        both = call(kernel, "beside_rows", arrays, outs, 3)
        sums, ahead = both["sums"], with_other("first", both["first"])
        diagonal, sums = lax.optimization_barrier((diagonal, sums))
        diagonal = with_other("diagonal", diagonal)
        if period == 0:
            seconds, sums = lax.optimization_barrier((seconds, sums))
            seconds[2] = lax.ppermute(seconds[2], "rows", across(count))
            seconds = with_other("seconds", jnp.concatenate(seconds, axis=0))
        arrays = common | diagonal | {"sums": sums}
        outs = {"out": tiles(2 * frames, channels)}
        middle = call(functools.partial(far_kernel, frames, base), "far_row", arrays, outs, 1)["out"]
        ahead, middle = lax.optimization_barrier((ahead, middle))
        kernel = functools.partial(second_ahead_kernel, frames, count)
        ahead = call(kernel, "second_ahead", common | ahead, {"ahead": tiles(frames, channels, F32)}, 1)
        arrays = common | with_other("middle", middle) | ahead | {"own": own["own"], "kept": first["kept"]}
        outs = {"out": tiles(frames, channels), "tails": tiles(2 * TAILS, channels)}
        if period:
            arrays |= {"older": out, "older_tails": tails, "cached_seconds": cached_seconds}
            if period < segments - 1:
                outs["result"] = tiles(frames, channels)
        else:
            arrays |= seconds
        second = call(functools.partial(second_kernel, frames, base, period, count), "second", arrays, outs, 3)
        out, tails = second["out"], second["tails"]
        if period < segments - 1:
            result = second["result"] if period else out
            source = lax.ppermute(result, "segment", [(i, (i + 1) % segments) for i in range(segments)])
            if period == 0:
                arrays, result = lax.optimization_barrier((common | own | beside | diagonal | seconds, result))
                outs = {"cached_sums": tiles(6, channels, F32), "cached_seconds": tiles(2, channels, F32)}
                sums = call(cached_kernel, "cached_rows", arrays, outs, 8)
                cached_sums, cached_seconds = sums["cached_sums"], sums["cached_seconds"]
                source, cached_sums, cached_seconds = lax.optimization_barrier((source, cached_sums, cached_seconds))
    return (out[None, :, None], tails.reshape(1, 2, 2, 1, channels, LANES))


def solution(mesh):
    in_specs = (
        P(None, "rows", "chan", None),
        P("segment", None, None, "rows", "chan", None),
        P("segment", None, "chan", None, None, None, None),
        P("segment", None, None),
        P("segment", None, None),
    )
    out_specs = (
        P("segment", None, "rows", "chan", None),
        P("segment", None, None, "rows", "chan", None),
    )
    return jax.shard_map(shards, mesh=mesh, in_specs=in_specs, out_specs=out_specs, check_vma=False)
```

```python
import functools

import jax
import jax.numpy as jnp
from jax import lax
from jax.experimental import pallas as pl
from jax.experimental.pallas import tpu as pltpu
from jax.sharding import PartitionSpec as P

BF16 = jnp.bfloat16
F32 = jnp.float32
LANES = 128
MIB = 1024 * 1024
VMEM = pl.BlockSpec(memory_space=pltpu.VMEM)
SMEM = pl.BlockSpec(memory_space=pltpu.SMEM)
TAILS = 2
FRAMES = 4


def params(mib):
    return pltpu.CompilerParams(vmem_limit_bytes=mib * MIB)


def turned(x, by):
    by = by % LANES
    return x if by == 0 else pltpu.roll(x, by, x.ndim - 1)


def tiles(count, channels, dtype=BF16):
    return jax.ShapeDtypeStruct((count, channels, LANES), dtype)


def prepared_kernel(place_ref, gain_ref, bias_ref, kernels_ref, gains_ref, biases_ref, all_ref):
    channels = biases_ref.shape[1]
    depth = gains_ref.shape[1]
    mine = pl.ds(pl.multiple_of(place_ref[0] * channels, channels), channels)
    for conv in range(2):
        for source, out in ((gain_ref, gains_ref.at[conv]), (bias_ref, all_ref)):
            for k in range(depth // LANES):
                at = slice(k * LANES, (k + 1) * LANES)
                out[at, :] = jnp.transpose(jnp.broadcast_to(source[conv : conv + 1, at], (LANES, LANES)))
        biases_ref[conv] = all_ref[mine, :]


def prepared(place, gain, bias, kernels, channels):
    depth = gain.shape[1]
    return pl.pallas_call(
        prepared_kernel,
        out_shape=(
            jax.ShapeDtypeStruct((2, depth, LANES), F32),
            jax.ShapeDtypeStruct((2, channels, LANES), F32),
        ),
        in_specs=[SMEM, VMEM, VMEM, VMEM],
        out_specs=(VMEM, VMEM),
        scratch_shapes=[pltpu.VMEM((depth, LANES), F32)],
        compiler_params=params(16),
        name="prepared",
    )(place, gain, bias, kernels)


class Part:
    def __init__(self, conv, ref):
        self.conv, self.ref = conv, ref
        self.window = ref["window"]
        self.weight = ref["weight"]
        _, self.taps, height, self.depth = self.weight.shape
        self.channels = height // 3
        self.mine_first = ref["place"][0] == 0
        self.side = ref["place"][1]
        self.lane = lax.broadcasted_iota(jnp.int32, (1, LANES), 1)

    def ordered(self, name, tile):
        own, other = self.ref[name][tile], self.ref[name + "_other"][tile]
        return [jnp.where(self.mine_first, own, other), jnp.where(self.mine_first, other, own)]

    def activate(self, slot, frame, name, tile, valid=None):
        values = [x.astype(F32) for x in self.ordered(name, tile)]
        square = sum(jnp.sum(v * v, axis=0, keepdims=True) for v in values)
        scale = 0.5 * lax.rsqrt(square / self.depth + 1e-06)
        if valid is not None:
            scale = jnp.where(valid, scale, 0.0)
        kept = []
        for h, value in enumerate(values):
            at = slice(h * self.channels, (h + 1) * self.channels)
            t = self.ref["gains"][self.conv, at, :] * value * scale
            active = (t + t * jnp.tanh(t)).astype(BF16)
            self.window[slot, frame + 2, at, :] = active
            kept.append(active)
        return jnp.where(self.mine_first, *kept)

    def cached(self, slot, name, tile):
        for f in range(2):
            for h, value in enumerate(self.ordered(name, tile + f)):
                self.window[slot, f, h * self.channels : (h + 1) * self.channels, :] = value

    def product(self, slots, first, frames, held=(True, True)):
        block, weight = [], []
        nothing = jnp.zeros((self.depth, LANES), BF16)
        for slot, tap, *held_here in slots:
            held_now = held_here[0] if held_here else held
            row_tap = 1 + self.side * (tap - 1)
            for a in range(3):
                wanted = [first + f + a for f in range(frames)]
                here = [held_now[0 if frame < 2 else 1] for frame in wanted]
                if any(here):
                    tile = [self.window[slot, frame] if h else nothing for frame, h in zip(wanted, here)]
                    weight.append(self.weight[self.conv, 3 * a + row_tap])
                    block.append(jnp.concatenate(tile, axis=1))
        total = jnp.dot(
            jnp.concatenate(weight, axis=1), jnp.concatenate(block, axis=0), preferred_element_type=F32
        )
        sums = []
        for f in range(frames):
            left, centre, right = [
                total[d * self.channels : (d + 1) * self.channels, f * LANES : (f + 1) * LANES] for d in range(3)
            ]
            left = jnp.where(self.lane == 0, 0.0, turned(left, 1))
            right = jnp.where(self.lane == LANES - 1, 0.0, turned(right, -1))
            sums.append(left + centre + right)
        return sums


def cached_kernel(names, *refs):
    ref = dict(zip(names, refs))
    first, second = Part(0, ref), Part(1, ref)
    held = (True, False)
    row = TAILS + FRAMES
    places = (("own", 0), ("beside", 0), ("pairs", 0), ("pairs", row), ("diagonal", 0))
    for slot, (name, tile) in enumerate(places):
        first.cached(slot, name, tile)
    for q, slots in ((-1, [(2, 0), (1, 1), (0, 2)]), (0, [(1, 0), (0, 1), (4, 2)]), (1, [(0, 0), (4, 1), (3, 2)])):
        for f, value in enumerate(first.product(slots, 0, 2, held)):
            ref["cached_sums"][2 * (q + 1) + f] = value + ref["biases"][0]
    for slot in range(3):
        second.cached(5 + slot, "seconds", TAILS * slot)
    for f, value in enumerate(second.product([(6, 0), (5, 1), (7, 2)], 0, 2, held)):
        ref["cached_seconds"][f] = value + ref["biases"][1]


def own_kernel(frames, base, names, *refs):
    ref = dict(zip(names, refs))
    part = Part(0, ref)
    half = frames // 2
    if base:
        part.cached(0, "own", 0)
    for first in (0, half):
        for f in range(first, first + half):
            kept = part.activate(0, f, "own", base + f)
            if f >= frames - 2:
                ref["kept"][f - frames + 2] = kept
        for q in (-1, 0, 1):
            for f, value in enumerate(part.product([(0, 1 - q)], first, half, (base > 0, True)), first):
                before = ref["biases"][0] if base or f >= 2 else ref["cached_sums"][2 * (q + 1) + f]
                ref["sums"][(q + 1) * frames + f] = value + before


def beside_kernel(frames, base, names, *refs):
    ref = dict(zip(names, refs))
    part = Part(0, ref)
    half = frames // 2
    places = (("beside", 0), ("pairs", 0), ("pairs", base + frames))

    def load(slot, first):
        name, tile = places[slot]
        if base and first == 0:
            part.cached(slot, name, tile)
        for f in range(first, first + half):
            part.activate(slot, f, name, tile + base + f)

    def store(q, slots, first):
        for f, value in enumerate(part.product(slots, first, half, (base > 0, True)), first):
            total = ref["sums_before"][(q + 1) * frames + f] + value
            if q < 0:
                ref["first"][f] = total.astype(BF16)
            else:
                ref["sums"][q * frames + f] = total

    for first in (0, half):
        load(0, first)
        store(0, [(0, 0)], first)
        load(1, first)
        store(-1, [(1, 0), (0, 1)], first)
        load(2, first)
        store(1, [(2, 2)], first)


def far_kernel(frames, base, names, *refs):
    ref = dict(zip(names, refs))
    part = Part(0, ref)
    half = frames // 2
    out, sums = ref["out"], ref["sums"]
    if base:
        part.cached(0, "diagonal", 0)
    for first in (0, half):
        for f in range(first, first + half):
            part.activate(0, f, "diagonal", base + f)
        for q, tap in ((0, 2), (1, 1)):
            for f, value in enumerate(part.product([(0, tap)], first, half, (base > 0, True)), first):
                at = q * frames + f
                out[at] = (sums[at] + value).astype(BF16)


def inside(part, count, q):
    at = part.ref["place"][2] + part.side * q
    return jnp.broadcast_to(jnp.logical_and(at >= 0, at < count), (1, LANES))


def second_ahead_kernel(frames, count, names, *refs):
    ref = dict(zip(names, refs))
    part = Part(1, ref)
    half = frames // 2
    for first in (0, half):
        for f in range(first, first + half):
            part.activate(0, f, "first", f, inside(part, count, -1))
        for f, value in enumerate(part.product([(0, 0)], first, half, (False, True)), first):
            ref["ahead"][f] = value


def second_kernel(frames, base, period, count, names, *refs):
    ref = dict(zip(names, refs))
    part = Part(1, ref)
    segment = ref["place"][3]
    bias = ref["biases"][1]
    half = frames // 2
    slots = [(0, 1), (1, 2)]
    if period == 0:
        for slot, place in enumerate((0, 2, 1)):
            part.cached(slot, "seconds", TAILS * place)
        slots.append((2, 0, (True, False)))
    tails = {f: ref["kept"][f] for f in range(2)}
    for first in (0, half):
        for q in range(2):
            for f in range(first, first + half):
                kept = part.activate(q, f, "middle", q * frames + f, inside(part, count, q) if q else None)
                if q == 0 and f >= frames - 2:
                    tails[4 + f - frames] = kept
        for f, value in enumerate(part.product(slots, first, half, (period == 0, True)), first):
            before = ref["cached_seconds"][f] if period and f < 2 else bias
            total = value + ref["ahead"][f] + before
            result = (ref["own"][base + f].astype(F32) + total).astype(BF16)
            if "result" in ref:
                ref["result"][f] = result
            ref["out"][f] = jnp.where(segment == period, result, ref["older"][f]) if period else result
    for f, tail in tails.items():
        ref["tails"][f] = jnp.where(segment == period, tail, ref["older_tails"][f]) if period else tail


TAKES = {"own_row": 3.0, "beside_rows": 3.7, "far_row": 2.3, "second_ahead": 1.6, "second": 3.0, "cached_rows": 4.0}


def call(kernel, name, arrays, outs, slots):
    depth = arrays["weight"].shape[-1]
    scratch = {"window": pltpu.VMEM((slots, FRAMES + 2, depth, LANES), BF16)}
    names = [*arrays, *outs, *scratch]
    results = pl.pallas_call(
        functools.partial(kernel, names),
        out_shape=list(outs.values()),
        in_specs=[SMEM if key == "place" else VMEM for key in arrays],
        out_specs=[VMEM] * len(outs),
        scratch_shapes=list(scratch.values()),
        compiler_params=params(16),
        cost_estimate=pl.CostEstimate(flops=int(TAKES[name] * 1.15e+09), transcendentals=0, bytes_accessed=0),
        name=name,
    )(*arrays.values())
    return dict(zip(outs, results))


def swapped(x):
    return lax.ppermute(x, "chan", [(0, 1), (1, 0)])


def with_other(name, x):
    return {name: x, name + "_other": swapped(x)}


def across(count):
    return [(i, i ^ 1) for i in range(count)]


def exchanged(x, count):
    pairs = count // 2
    even, odd = [], []
    for i in range(count):
        k = i // 2
        for k_to, group in ((k ^ 1, odd), (k + 1 if k % 2 else k - 1, even)):
            if 0 <= k_to < pairs:
                group.append((i, 2 * k_to + i % 2))
    return [lax.ppermute(x, "rows", pairs) for pairs in (across(count), even, odd)]


def shards(features, caches, conv_weights, conv_bias, norm_gain):
    count = lax.axis_size("rows")
    segments = lax.axis_size("segment")
    row = lax.axis_index("rows")
    frames, _, channels, _ = features.shape
    depth = conv_weights.shape[-1]
    kernels = jnp.transpose(conv_weights[0], (0, 2, 3, 4, 1, 5)).reshape(2, 9, 3 * channels, depth)
    kind, pair = row % 2, row // 2
    place = [lax.axis_index("chan"), 2 * kind - 1, row, lax.axis_index("segment")]
    place = jnp.stack(place).astype(jnp.int32)

    source = jnp.concatenate([caches[0].reshape(2 * TAILS, channels, LANES), features[:, 0]], axis=0)
    gains, biases = prepared(place, norm_gain[0], conv_bias[0], kernels, channels)
    source = jnp.concatenate([caches[0].reshape(2 * TAILS, channels, LANES), features[:, 0]], axis=0)
    sums_shape, kept_shape = tiles(3 * frames, channels, F32), tiles(2, channels)
    near_first = kind != pair % 2
    out = tails = cached_seconds = None
    for period in range(segments):
        base = 0 if period else TAILS
        beside, even, odd = exchanged(source, count)
        if period == 0:
            even, odd, gains, biases = lax.optimization_barrier((even, odd, gains, biases))
            common = {"place": place, "gains": gains, "biases": biases, "weight": kernels}
        near, far = jnp.where(near_first, even, odd), jnp.where(near_first, odd, even)
        if period == 0:
            seconds = [x[TAILS : 2 * TAILS] for x in (source, beside, near)]
            source, beside, near, far = [
                jnp.concatenate([x[:TAILS], x[2 * TAILS :]], axis=0) for x in (source, beside, near, far)
            ]
        own = with_other("own", source)
        diagonal = lax.ppermute(near, "rows", across(count))
        pairs = jnp.concatenate([near, far], axis=0)
        own["own_other"], beside, pairs = lax.optimization_barrier((own["own_other"], beside, pairs))
        beside = with_other("beside", beside) | with_other("pairs", pairs)
        arrays = common | own | ({"cached_sums": cached_sums} if period else {})
        outs = {"sums": sums_shape, "kept": kept_shape}
        first = call(functools.partial(own_kernel, frames, base), "own_row", arrays, outs, 1)
        arrays = common | beside | {"sums_before": first["sums"]}
        kernel = functools.partial(beside_kernel, frames, base)
        outs = {"sums": tiles(2 * frames, channels, F32), "first": tiles(frames, channels)}
        both = call(kernel, "beside_rows", arrays, outs, 3)
        sums, ahead = both["sums"], with_other("first", both["first"])
        diagonal, sums = lax.optimization_barrier((diagonal, sums))
        diagonal = with_other("diagonal", diagonal)
        if period == 0:
            seconds, sums = lax.optimization_barrier((seconds, sums))
            seconds[2] = lax.ppermute(seconds[2], "rows", across(count))
            seconds = with_other("seconds", jnp.concatenate(seconds, axis=0))
        arrays = common | diagonal | {"sums": sums}
        outs = {"out": tiles(2 * frames, channels)}
        middle = call(functools.partial(far_kernel, frames, base), "far_row", arrays, outs, 1)["out"]
        ahead, middle = lax.optimization_barrier((ahead, middle))
        kernel = functools.partial(second_ahead_kernel, frames, count)
        ahead = call(kernel, "second_ahead", common | ahead, {"ahead": tiles(frames, channels, F32)}, 1)
        arrays = common | with_other("middle", middle) | ahead | {"own": own["own"], "kept": first["kept"]}
        outs = {"out": tiles(frames, channels), "tails": tiles(2 * TAILS, channels)}
        if period:
            arrays |= {"older": out, "older_tails": tails, "cached_seconds": cached_seconds}
            if period < segments - 1:
                outs["result"] = tiles(frames, channels)
        else:
            arrays |= seconds
        second = call(functools.partial(second_kernel, frames, base, period, count), "second", arrays, outs, 3)
        out, tails = second["out"], second["tails"]
        if period < segments - 1:
            result = second["result"] if period else out
            source = lax.ppermute(result, "segment", [(i, (i + 1) % segments) for i in range(segments)])
            if period == 0:
                arrays, result = lax.optimization_barrier((common | own | beside | diagonal | seconds, result))
                outs = {"cached_sums": tiles(6, channels, F32), "cached_seconds": tiles(2, channels, F32)}
                sums = call(cached_kernel, "cached_rows", arrays, outs, 8)
                cached_sums, cached_seconds = sums["cached_sums"], sums["cached_seconds"]
                source, cached_sums, cached_seconds = lax.optimization_barrier((source, cached_sums, cached_seconds))
    return (out[None, :, None], tails.reshape(1, 2, 2, 1, channels, LANES))


def solution(mesh):
    in_specs = (
        P(None, "rows", "chan", None),
        P("segment", None, None, "rows", "chan", None),
        P("segment", None, "chan", None, None, None, None),
        P("segment", None, None),
        P("segment", None, None),
    )
    out_specs = (
        P("segment", None, "rows", "chan", None),
        P("segment", None, None, "rows", "chan", None),
    )
    return jax.shard_map(shards, mesh=mesh, in_specs=in_specs, out_specs=out_specs, check_vma=False)
```
